128 devices in a mesh: gauss: 16 (over y_hi, z, core), img: 8 (over y_lo, x).
Axes of the slice: x: 4, y: 4 (y_hi: 2, y_lo: 2; y = y_hi * 2 + y_lo), z: 4, core: 2. Of those that a mesh axis runs over, the one named last changes fastest.
Arguments:
- observed: bfloat16 [32, 256, 256], P('img', 'gauss'), may hold values from -6 to 6
- pose_index: int32 [32], P('img'), may hold values from 0 to 4095
- batch_order: int32 [32], P('img'), may hold values from 0 to 3, as said below
- latents: float32 [32, 16], P('img'), may hold values from -3 to 3
- base_positions: float32 [3, 131072], P(None, 'gauss'), may hold values from -70 to 69
- amplitudes: float32 [131072], P('gauss'), may hold values from -0.875 to 0.875
- widths: float32 [131072], P('gauss'), may hold values from 1 to 3
- deform_modes: float32 [16, 3, 131072], P(None, None, ('gauss', 'img')), may hold values from -12 to 12
Outputs:
- final_residual: float32 [8, 256, 256], P('img', 'gauss')
- new_modes: float32 [16, 3, 131072], P(None, None, ('gauss', 'img'))
The draws below stay inside these ranges and needn't reach their ends.
Inputs may be any that keep to these rules, and one draw needn't show every extreme that they name: `batch_order`: in each aligned block of 4 entries (one device's images) every number from 0 to 3 appears exactly once.
All inputs are finite; a program needn't handle non-finite values.
Results may differ from the reference program's by a relative error of at most 0.0045.
Values may be sent and summed in bfloat16 or wider, within the bound.
A program may use at most 64 MiB of HBM per device.

```python
import math
import jax
import jax.numpy as jnp
from jax import lax

PIX = 256
K = 16
NROT = 4096
STEPS = 2
IMG_DEV = 4
G_DEV = 8192
GAUSSIANS = 131072
IMAGES = 32
BATCH = 8


def draw_batch_order(key, part):
    keys = jax.random.split(key, IMAGES // IMG_DEV)
    orders = jax.vmap(lambda one_key: jax.random.permutation(one_key, IMG_DEV))(keys)
    return orders.reshape(-1).astype(jnp.int32)


def set_ends(entries, stream_key, least, largest):
    extent = entries.shape
    place = [jax.random.randint(jax.random.fold_in(stream_key, axis), (), 0, extent[axis]) for axis in range(len(extent))]
    entries = entries.at[tuple(place)].set(least)
    longest = extent.index(max(extent))
    place[longest] = (place[longest] + 1) % extent[longest]
    return entries.at[tuple(place)].set(largest)


def levels(own_key, shape, cuts, low, largest):
    def one(axis_at, shards_of):
        draws = jax.random.uniform(jax.random.fold_in(jax.random.fold_in(own_key, 6), axis_at), (shards_of,), jnp.float32, low / len(cuts), largest / len(cuts))
        return jnp.repeat(jnp.exp(draws), shape[axis_at] // shards_of).reshape((-1,) + (1,) * (len(shape) - axis_at - 1))

    loudness = one(*cuts[0])
    for cut in cuts[1:]:
        loudness = loudness * one(*cut)
    return loudness


def scatter_about(stream_key, dims, spread, bound, cuts=(), kind=jnp.bfloat16):
    values = spread * jax.random.normal(stream_key, dims, jnp.float32)
    if cuts:
        values = values * levels(stream_key, dims, cuts, -0.22, 0.18)
    return jnp.clip(values, -bound, bound).astype(kind)


def setup_inputs(seed: int = 0) -> dict:
    key_of = jax.random.split(jax.random.key(seed), 9)
    return {
        "observed": scatter_about(key_of[0], (IMAGES, PIX, PIX), 1.0, 6.0, ((0, 8), (1, 16))),
        "pose_index": set_ends(jax.random.randint(key_of[1], (IMAGES,), 0, NROT), jax.random.fold_in(key_of[1], 1), 0, NROT - 1).astype(jnp.int32),
        "batch_order": draw_batch_order(jax.random.fold_in(key_of[8], 71), 0),
        "latents": scatter_about(key_of[3], (IMAGES, K), 0.5, 3.0, ((0, 8),), jnp.float32),
        "base_positions": jnp.clip(-70.0 + 139.0 * jax.random.uniform(key_of[4], (3, GAUSSIANS), jnp.float32) ** levels(key_of[4], (3, GAUSSIANS), ((1, 16),), -0.2, 0.2), -70.0, 69.0),
        "amplitudes": scatter_about(key_of[5], (GAUSSIANS,), (24 * GAUSSIANS // (PIX * PIX)) ** -0.5, 0.875, ((0, 16),), jnp.float32),
        "widths": jnp.clip(jnp.exp(math.log(3.0) - 1.0986123 * jax.random.uniform(key_of[6], (GAUSSIANS,), jnp.float32) ** levels(key_of[6], (GAUSSIANS,), ((0, 16),), -0.2, 0.2)), 1.0, 3.0),
        "deform_modes": scatter_about(key_of[7], (K, 3, GAUSSIANS), 2.0, 12.0, ((2, 128),), jnp.float32),
    }


step_size = 0.5
tiny_eps = 1e-06

def rotation_rows(pose_id):
    cos_beta = 1.0 - (2 * pose_id + 1).astype(jnp.float32) / NROT
    sin_beta = jnp.sqrt(1.0 - cos_beta * cos_beta)
    alpha = (pose_id * 55 % 144).astype(jnp.float32) * (2.0 * math.pi / 144.0)
    gamma = (pose_id % 8).astype(jnp.float32) * (math.pi / 4.0)
    cos_alpha, sin_alpha = (jnp.cos(alpha), jnp.sin(alpha))
    cos_gamma, sin_gamma = (jnp.cos(gamma), jnp.sin(gamma))
    first = jnp.stack([cos_alpha * cos_beta * cos_gamma - sin_alpha * sin_gamma, -cos_alpha * cos_beta * sin_gamma - sin_alpha * cos_gamma, cos_alpha * sin_beta])
    second = jnp.stack([sin_alpha * cos_beta * cos_gamma + cos_alpha * sin_gamma, -sin_alpha * cos_beta * sin_gamma + cos_alpha * cos_gamma, sin_alpha * sin_beta])
    return jnp.stack([first, second])

def factors(positions, rotation, amplitudes, widths):
    center = (PIX - 1) * 0.5
    proj_u = rotation[0, 0] * positions[0] + rotation[0, 1] * positions[1] + rotation[0, 2] * positions[2] + center
    proj_v = rotation[1, 0] * positions[0] + rotation[1, 1] * positions[1] + rotation[1, 2] * positions[2] + center
    pixels = jnp.arange(PIX).astype(jnp.float32)
    inv_var = 1.0 / (widths * widths)
    diff_u = pixels[None, :] - proj_u[:, None]
    diff_v = pixels[None, :] - proj_v[:, None]
    profile_u = jnp.exp(-0.5 * diff_u * diff_u * inv_var[:, None]).astype(jnp.bfloat16)
    profile_v = (amplitudes[:, None] * jnp.exp(-0.5 * diff_v * diff_v * inv_var[:, None])).astype(jnp.bfloat16)
    return (profile_u, profile_v, diff_u, diff_v, inv_var)

def block_grads(positions, rotation, amplitudes, widths, residual_b):
    profile_u, profile_v, diff_u, diff_v, inv_var = factors(positions, rotation, amplitudes, widths)
    pu = profile_u.astype(jnp.float32)
    pv = profile_v.astype(jnp.float32)
    rb = residual_b.astype(jnp.float32)
    weighted_u = jnp.dot(pv, rb.T, precision=lax.Precision.HIGHEST, preferred_element_type=jnp.float32)
    weighted_v = jnp.dot(pu, rb, precision=lax.Precision.HIGHEST, preferred_element_type=jnp.float32)
    grad_u = inv_var * lax.optimization_barrier(jnp.sum(pu * diff_u * weighted_u, axis=1))
    grad_v = inv_var * lax.optimization_barrier(jnp.sum(pv * diff_v * weighted_v, axis=1))
    return jnp.stack([rotation[0, c] * grad_u + rotation[1, c] * grad_v for c in range(3)])

def reference(observed, pose_index, batch_order, latents, base_positions, amplitudes, widths, deform_modes):
    blocks = GAUSSIANS // G_DEV
    amp_blocks = amplitudes.reshape(blocks, G_DEV)
    wid_blocks = widths.reshape(blocks, G_DEV)
    current = deform_modes
    finals = []
    for outer in range(STEPS):
        mode_grad = jnp.zeros((K, 3, GAUSSIANS), jnp.float32)
        finals = []
        for member in range(BATCH):
            chosen = member * IMG_DEV + batch_order[member * IMG_DEV + outer]
            rotation = rotation_rows(pose_index[chosen])
            latent = latents[chosen]
            positions = base_positions + jnp.einsum('k,kcg->cg', latent, current, precision=lax.Precision.HIGHEST)
            pos_blocks = positions.reshape(3, blocks, G_DEV).transpose(1, 0, 2)

            def add_block(running, pieces):
                profile_u, profile_v, diff_u, diff_v, inv_var = factors(pieces[0], rotation, pieces[1], pieces[2])
                term = jnp.dot(profile_u.astype(jnp.float32).T, profile_v.astype(jnp.float32), precision=lax.Precision.HIGHEST, preferred_element_type=jnp.float32)
                return (running + term, None)
            image, unused = lax.scan(add_block, jnp.zeros((PIX, PIX), jnp.float32), (pos_blocks, amp_blocks, wid_blocks))
            residual = image - observed[chosen].astype(jnp.float32)
            residual_b = residual.astype(jnp.bfloat16)
            shift_blocks = lax.map(lambda pieces: block_grads(pieces[0], rotation, pieces[1], pieces[2], residual_b), (pos_blocks, amp_blocks, wid_blocks))
            shift_grad = shift_blocks.transpose(1, 0, 2).reshape(3, GAUSSIANS)
            mode_grad = mode_grad + latent[:, None, None] * shift_grad[None]
            finals.append(residual)
        squares = jnp.sum(mode_grad * mode_grad)
        current = current - step_size * mode_grad / jnp.sqrt(squares / (3 * K * GAUSSIANS) + tiny_eps)
    return (jnp.stack(finals), current)
```

```python
import functools
import math

import jax
import jax.numpy as jnp
from jax import lax
from jax.experimental import pallas as pl
from jax.experimental.pallas import tpu as pltpu
from jax.sharding import PartitionSpec as P

PIX = 256
K = 16
NROT = 4096
STEPS = 2
SUB = 1024
TILES = SUB // 128
BLK = 256
CENTER = (PIX - 1) * 0.5

step_size = 0.5
tiny_eps = 1e-06
MESH = pl.DeviceIdType.MESH
HIGH = lax.Precision.HIGHEST


def cos_sin(units):
    quarter = (
        (units >= 18).astype(jnp.int32)
        + (units >= 54).astype(jnp.int32)
        + (units >= 90).astype(jnp.int32)
        + (units >= 126).astype(jnp.int32)
    )
    x = (units - 36 * quarter).astype(jnp.float32) * (2.0 * math.pi / 144.0)
    y = x * x
    s = x * (1.0 + y * (-1.0 / 6 + y * (1.0 / 120 + y * (-1.0 / 5040 + y * (1.0 / 362880)))))
    c = 1.0 + y * (
        -0.5 + y * (1.0 / 24 + y * (-1.0 / 720 + y * (1.0 / 40320 - y * (1.0 / 3628800))))
    )
    odd = (quarter == 1) | (quarter == 3)
    cos_a = jnp.where(odd, s, c)
    sin_a = jnp.where(odd, c, s)
    cos_a = jnp.where((quarter == 1) | (quarter == 2), -cos_a, cos_a)
    sin_a = jnp.where((quarter == 2) | (quarter == 3), -sin_a, sin_a)
    return cos_a, sin_a


def own_coefficients(pose, latent):
    lane = lax.broadcasted_iota(jnp.int32, (1, 128), 1)
    n = jnp.full((1, 128), pose, jnp.int32)
    cos_b = 1.0 - (2 * n + 1).astype(jnp.float32) * (1.0 / NROT)
    sin_b = jnp.sqrt(1.0 - cos_b * cos_b)
    cos_a, sin_a = cos_sin(jnp.full((1, 128), lax.rem(pose * 55, 144), jnp.int32))
    cos_g, sin_g = cos_sin(jnp.full((1, 128), lax.rem(pose, 8) * 18, jnp.int32))
    rows = (
        (
            cos_a * cos_b * cos_g - sin_a * sin_g,
            -cos_a * cos_b * sin_g - sin_a * cos_g,
            cos_a * sin_b,
        ),
        (
            sin_a * cos_b * cos_g + cos_a * sin_g,
            -sin_a * cos_b * sin_g + cos_a * cos_g,
            sin_a * sin_b,
        ),
    )
    spread = latent + pltpu.roll(latent, K, 1) + pltpu.roll(latent, 2 * K, 1)
    spread = jnp.where(lane < 3 * K, spread, jnp.where(lane < 3 * K + 3, 1.0, 0.0))
    first = (lane < K) | (lane == 3 * K)
    second = ((lane >= K) & (lane < 2 * K)) | (lane == 3 * K + 1)
    return [spread * jnp.where(first, r[0], jnp.where(second, r[1], r[2])) for r in rows]


def kernel(
    ng,
    ni,
    pose_ref,
    order_ref,
    lat_ref,
    obs_hbm,
    base_hbm,
    amp_hbm,
    wid_hbm,
    modes_hbm,
    res_hbm,
    new_hbm,
    zpad,
    obs,
    rows_in,
    base_in,
    amp,
    wid,
    curve,
    psend,
    params,
    xbuf,
    asend,
    arecv,
    bsend,
    brecv,
    proj,
    pu,
    pv,
    image,
    isend,
    irecv,
    resid,
    rsend,
    whole,
    whole_t,
    grads,
    gsend,
    grecv,
    mgrad,
    s1,
    s2send,
    s2,
    newv,
    in_sem,
    out_sem,
    p_sem,
    a_sem,
    b_sem,
    i_sem,
    r_sem,
    g_sem,
    s1_sem,
    s2_sem,
):
    rows = PIX // ng
    blocks = ni * SUB // BLK
    per_sub = SUB // BLK
    entries = 3 * K * SUB * ni * ng
    gj = lax.axis_index("gauss")
    ib = lax.axis_index("img")

    loads = [
        pltpu.make_async_copy(modes_hbm, rows_in.at[pl.ds(0, 3 * K)], in_sem.at[0]),
        pltpu.make_async_copy(
            base_hbm.at[:, pl.ds(pl.multiple_of(ib * SUB, SUB), SUB)], base_in, in_sem.at[1]
        ),
        pltpu.make_async_copy(amp_hbm, amp, in_sem.at[2]),
        pltpu.make_async_copy(wid_hbm, wid, in_sem.at[3]),
        pltpu.make_async_copy(obs_hbm, obs, in_sem.at[4]),
    ]
    for copy in loads:
        copy.start()

    barrier = pltpu.get_barrier_semaphore()
    for axis, me, n in (("img", ib, ni), ("gauss", gj, ng)):
        for r in range(1, n):
            pl.semaphore_signal(
                barrier, inc=1, device_id={axis: lax.rem(me + r, n)}, device_id_type=MESH
            )

    zpad[...] = jnp.zeros_like(zpad)
    zpad[0:4, 0:K] = lat_ref[...]
    chosen = [order_ref[s] for s in range(STEPS)]
    psend[...] = jnp.zeros_like(psend)
    for s in range(STEPS):
        both = own_coefficients(pose_ref[chosen[s]], zpad[pl.ds(chosen[s], 1), :])
        psend[2 * s : 2 * s + 1, :] = both[0]
        psend[2 * s + 1 : 2 * s + 2, :] = both[1]
    params[ib] = psend[...]

    pl.semaphore_wait(barrier, ni + ng - 2)

    def send_all(axis, source, target, sem):
        me, n = (ib, ni) if axis == "img" else (gj, ng)
        for r in range(1, n):
            peer = lax.rem(me + r, n)
            pltpu.make_async_remote_copy(
                src_ref=source(peer),
                dst_ref=target(me, r),
                send_sem=sem.at[0],
                recv_sem=sem.at[1],
                device_id={axis: peer},
                device_id_type=MESH,
            ).start()

    def wait_for(part, sem):
        pltpu.make_async_copy(part, part, sem).wait()

    send_all("img", lambda peer: psend, lambda me, r: params.at[me], p_sem)

    loads[0].wait()
    loads[1].wait()
    rows_in[3 * K :, :] = jnp.zeros_like(rows_in[3 * K :, :])
    rows_in[3 * K : 3 * K + 3, :] = base_in[...]
    loads[3].wait()
    w = wid[...]
    inv = 1.0 / (w * w)
    curve[1] = inv
    curve[0] = inv * (-0.5 * math.log2(math.e))

    wait_for(params.at[pl.ds(0, ni - 1)], p_sem.at[1])

    def coefficients(s):
        return jnp.concatenate([params[:, 2 * s, :], params[:, 2 * s + 1, :]], axis=0)

    def project(s, source, center, target):
        got = lax.dot_general(
            coefficients(s)[:, : source.shape[0]],
            source,
            (((1,), (0,)), ((), ())),
            precision=HIGH,
            preferred_element_type=jnp.float32,
        )
        if center:
            got = got + CENTER
        for t in range(TILES):
            xbuf[t] = got[:, t * 128 : (t + 1) * 128]
        for b in range(ni):
            for uv in range(2):
                target[b, uv] = xbuf[:, uv * ni + b, :]

    project(0, rows_in[...], True, asend.at[0])
    send_all("img", lambda peer: asend.at[0, peer], lambda me, r: arecv.at[0, me], a_sem.at[0])
    arecv[0, ib] = asend[0, ib]
    project(1, rows_in[...], True, asend.at[1])
    send_all("img", lambda peer: asend.at[1, peer], lambda me, r: arecv.at[1, me], a_sem.at[1])
    arecv[1, ib] = asend[1, ib]
    loads[2].wait()
    wait_for(arecv.at[0, pl.ds(0, ni - 1)], a_sem.at[0, 1])

    pixel16 = lax.broadcasted_iota(jnp.int32, (16, 128), 0).astype(jnp.float32)
    halves = []

    for s in range(STEPS):
        if s == 0:
            proj[...] = arecv[0]
        else:
            wait_for(arecv.at[1, pl.ds(0, ni - 1)], a_sem.at[1, 1])
            wait_for(brecv.at[pl.ds(0, ni - 1)], b_sem.at[1])
            proj[...] = arecv[1] - halves[0] * brecv[...]

        image[...] = jnp.zeros_like(image)

        def render(i, carry):
            b = i // per_sub
            t0 = (i % per_sub) * (BLK // 128)
            for tt in range(BLK // 128):
                g = b * TILES + t0 + tt
                c = curve[0, pl.ds(g, 1), :]
                a = amp[pl.ds(g, 1), :]
                lanes = slice(tt * 128, (tt + 1) * 128)
                du = pixel16 - proj[b, 0, pl.ds(t0 + tt, 1), :]
                dv = pixel16 - proj[b, 1, pl.ds(t0 + tt, 1), :]
                for m in range(PIX // 16):
                    d = du + 16.0 * m
                    pu[i, m * 16 : (m + 1) * 16, lanes] = jnp.exp2(d * d * c).astype(jnp.bfloat16)
                    d = dv + 16.0 * m
                    pv[i, m * 16 : (m + 1) * 16, lanes] = (a * jnp.exp2(d * d * c)).astype(
                        jnp.bfloat16
                    )
            image[...] += lax.dot_general(
                pu[i],
                pv[i],
                (((1,), (1,)), ((), ())),
                preferred_element_type=jnp.float32,
            )
            return carry

        lax.fori_loop(0, blocks, render, 0)

        for j in range(ng):
            isend[s, j] = image[j * rows : (j + 1) * rows, :].astype(isend.dtype)
        send_all(
            "gauss",
            lambda peer: isend.at[s, peer],
            lambda me, r: irecv.at[s, r - 1],
            i_sem.at[s],
        )
        if s == 0:
            loads[4].wait()
        measured = obs[chosen[s]].astype(jnp.float32)
        total = image[pl.ds(pl.multiple_of(gj * rows, rows), rows), :] - measured
        wait_for(irecv.at[s], i_sem.at[s, 1])
        for r in range(ng - 1):
            total = total + irecv[s, r].astype(jnp.float32)
        rsend[s] = total.astype(jnp.bfloat16)
        send_all("gauss", lambda peer: rsend.at[s], lambda me, r: whole.at[s, me], r_sem.at[s])
        whole[s, gj] = rsend[s]
        if s == STEPS - 1:
            resid[...] = total
            pltpu.make_async_copy(resid, res_hbm, out_sem.at[0]).start()
        wait_for(whole.at[s, pl.ds(0, ng - 1)], r_sem.at[s, 1])
        whole_t[0] = whole[s].reshape(PIX, PIX)
        whole_t[1] = whole_t[0].T

        def backward(i, carry):
            b = i // per_sub
            t0 = (i % per_sub) * (BLK // 128)
            sides = ((0, pu, whole_t[0], pv), (1, pv, whole_t[1], pu))
            for uv, own, matrix, other in sides:
                weighted = jnp.dot(matrix, other[i], preferred_element_type=jnp.float32)
                for tt in range(BLK // 128):
                    g = b * TILES + t0 + tt
                    lanes = slice(tt * 128, (tt + 1) * 128)
                    d0 = pixel16 - proj[b, uv, pl.ds(t0 + tt, 1), :]
                    total = jnp.zeros((16, 128), jnp.float32)
                    for m in range(PIX // 16):
                        span = slice(m * 16, (m + 1) * 16)
                        total += (
                            own[i, span, lanes].astype(jnp.float32)
                            * (d0 + 16.0 * m)
                            * weighted[span, lanes]
                        )
                    gsend[s, b, uv, pl.ds(t0 + tt, 1), :] = curve[1, pl.ds(g, 1), :] * jnp.sum(
                        total, axis=0, keepdims=True
                    )
            return carry

        lax.fori_loop(0, blocks, backward, 0)

        send_all("img", lambda peer: gsend.at[s, peer], lambda me, r: grecv.at[s, me], g_sem.at[s])
        grecv[s, ib] = gsend[s, ib]
        wait_for(grecv.at[s, pl.ds(0, ni - 1)], g_sem.at[s, 1])
        for uv in range(2):
            for t in range(TILES):
                grads[uv * ni : (uv + 1) * ni, t * 128 : (t + 1) * 128] = grecv[s, :, uv, t, :]
        got = lax.dot_general(
            coefficients(s)[:, : 3 * K],
            grads[...],
            (((0,), (0,)), ((), ())),
            precision=HIGH,
            preferred_element_type=jnp.float32,
        )
        mgrad[s] = got
        squares = jnp.zeros((8, 128), jnp.float32)
        for k in range(3 * K // 8):
            for t in range(TILES):
                part = got[k * 8 : (k + 1) * 8, t * 128 : (t + 1) * 128]
                squares = squares + part * part
        s1[s, ib] = squares
        send_all("img", lambda peer: s1.at[s, ib], lambda me, r: s1.at[s, me], s1_sem.at[s])
        if s == 0:
            project(1, mgrad[0], False, bsend)
            send_all("img", lambda peer: bsend.at[peer], lambda me, r: brecv.at[me], b_sem)
            brecv[ib] = bsend[ib]
        wait_for(s1.at[s, pl.ds(0, ni - 1)], s1_sem.at[s, 1])
        s2[s, gj] = jnp.sum(s1[s], axis=0)
        send_all("gauss", lambda peer: s2.at[s, gj], lambda me, r: s2.at[s, me], s2_sem.at[s])
        wait_for(s2.at[s, pl.ds(0, ng - 1)], s2_sem.at[s, 1])
        sums = jnp.sum(s2[s], axis=0)
        sums = jnp.sum(jnp.sum(sums, axis=0, keepdims=True), axis=1, keepdims=True)
        halves.append(step_size / jnp.sqrt(sums * (1.0 / entries) + tiny_eps))

    newv[...] = rows_in[: 3 * K, :] - halves[0] * mgrad[0] - halves[1] * mgrad[1]
    done = pltpu.make_async_copy(newv, new_hbm, out_sem.at[1])
    done.start()

    wait_for(params.at[pl.ds(0, ni - 1)], p_sem.at[0])
    wait_for(brecv.at[pl.ds(0, ni - 1)], b_sem.at[0])
    for s in range(STEPS):
        wait_for(arecv.at[s, pl.ds(0, ni - 1)], a_sem.at[s, 0])
        wait_for(irecv.at[s], i_sem.at[s, 0])
        wait_for(whole.at[s, pl.ds(0, ng - 1)], r_sem.at[s, 0])
        wait_for(grecv.at[s, pl.ds(0, ni - 1)], g_sem.at[s, 0])
        wait_for(s1.at[s, pl.ds(0, ni - 1)], s1_sem.at[s, 0])
        wait_for(s2.at[s, pl.ds(0, ng - 1)], s2_sem.at[s, 0])
    pltpu.make_async_copy(resid, res_hbm, out_sem.at[0]).wait()
    done.wait()


def body(
    observed, pose_index, batch_order, latents, base_positions, amplitudes, widths, deform_modes
):
    ng, ni = lax.axis_size("gauss"), lax.axis_size("img")
    rows = PIX // ng
    count = ni * SUB
    blocks = count // BLK
    f32, b16 = jnp.float32, jnp.bfloat16
    vmem, hbm, smem = (
        pl.BlockSpec(memory_space=m) for m in (pltpu.VMEM, pl.ANY, pltpu.SMEM)
    )
    dma = pltpu.SemaphoreType.DMA
    final, new = pl.pallas_call(
        functools.partial(kernel, ng, ni),
        out_shape=(
            jax.ShapeDtypeStruct((rows, PIX), f32),
            jax.ShapeDtypeStruct((3 * K, SUB), f32),
        ),
        in_specs=[smem, smem, vmem, hbm, hbm, hbm, hbm, hbm],
        out_specs=(hbm, hbm),
        scratch_shapes=[
            pltpu.VMEM((8, 128), f32),
            pltpu.VMEM((4, rows, PIX), b16),
            pltpu.VMEM((3 * K + 8, SUB), f32),
            pltpu.VMEM((3, SUB), f32),
            pltpu.VMEM((count // 128, 128), f32),
            pltpu.VMEM((count // 128, 128), f32),
            pltpu.VMEM((2, count // 128, 128), f32),
            pltpu.VMEM((8, 128), f32),
            pltpu.VMEM((ni, 8, 128), f32),
            pltpu.VMEM((TILES, 2 * ni, 128), f32),
            pltpu.VMEM((STEPS, ni, 2, TILES, 128), f32),
            pltpu.VMEM((STEPS, ni, 2, TILES, 128), f32),
            pltpu.VMEM((ni, 2, TILES, 128), f32),
            pltpu.VMEM((ni, 2, TILES, 128), f32),
            pltpu.VMEM((ni, 2, TILES, 128), f32),
            pltpu.VMEM((blocks, PIX, BLK), b16),
            pltpu.VMEM((blocks, PIX, BLK), b16),
            pltpu.VMEM((PIX, PIX), f32),
            pltpu.VMEM((STEPS, ng, rows, PIX), b16),
            pltpu.VMEM((STEPS, ng - 1, rows, PIX), b16),
            pltpu.VMEM((rows, PIX), f32),
            pltpu.VMEM((STEPS, rows, PIX), b16),
            pltpu.VMEM((STEPS, ng, rows, PIX), b16),
            pltpu.VMEM((2, PIX, PIX), b16),
            pltpu.VMEM((2 * ni, SUB), f32),
            pltpu.VMEM((STEPS, ni, 2, TILES, 128), f32),
            pltpu.VMEM((STEPS, ni, 2, TILES, 128), f32),
            pltpu.VMEM((STEPS, 3 * K, SUB), f32),
            pltpu.VMEM((STEPS, ni, 8, 128), f32),
            pltpu.VMEM((8, 128), f32),
            pltpu.VMEM((STEPS, ng, 8, 128), f32),
            pltpu.VMEM((3 * K, SUB), f32),
            dma((5,)),
            dma((2,)),
            dma((2,)),
            dma((STEPS, 2)),
            dma((2,)),
            dma((STEPS, 2)),
            dma((STEPS, 2)),
            dma((STEPS, 2)),
            dma((STEPS, 2)),
            dma((STEPS, 2)),
        ],
        compiler_params=pltpu.CompilerParams(
            collective_id=0, has_side_effects=True, vmem_limit_bytes=48 * 2**20
        ),
    )(
        pose_index,
        batch_order,
        latents,
        observed,
        base_positions,
        amplitudes.reshape(count // 128, 128),
        widths.reshape(count // 128, 128),
        deform_modes.transpose(1, 0, 2).reshape(3 * K, SUB),
    )
    return final[None], new.reshape(3, K, SUB).transpose(1, 0, 2)


def solution(mesh):
    return jax.shard_map(
        body,
        mesh=mesh,
        in_specs=(
            P("img", "gauss", None),
            P("img"),
            P("img"),
            P("img", None),
            P(None, "gauss"),
            P("gauss"),
            P("gauss"),
            P(None, None, ("gauss", "img")),
        ),
        out_specs=(P("img", "gauss", None), P(None, None, ("gauss", "img"))),
        check_vma=False,
    )
```

```python
import functools
import math

import jax
import jax.numpy as jnp
from jax import lax
from jax.experimental import pallas as pl
from jax.experimental.pallas import tpu as pltpu
from jax.sharding import PartitionSpec as P

PIX = 256
K = 16
NROT = 4096
STEPS = 2
SUB = 1024
TILES = SUB // 128
BLK = 512
CENTER = (PIX - 1) * 0.5

step_size = 0.5
tiny_eps = 1e-06
MESH = pl.DeviceIdType.MESH
HIGH = lax.Precision.HIGHEST


def cos_sin(units):
    quarter = (
        (units >= 18).astype(jnp.int32)
        + (units >= 54).astype(jnp.int32)
        + (units >= 90).astype(jnp.int32)
        + (units >= 126).astype(jnp.int32)
    )
    x = (units - 36 * quarter).astype(jnp.float32) * (2.0 * math.pi / 144.0)
    y = x * x
    s = x * (1.0 + y * (-1.0 / 6 + y * (1.0 / 120 + y * (-1.0 / 5040 + y * (1.0 / 362880)))))
    c = 1.0 + y * (
        -0.5 + y * (1.0 / 24 + y * (-1.0 / 720 + y * (1.0 / 40320 - y * (1.0 / 3628800))))
    )
    odd = (quarter == 1) | (quarter == 3)
    cos_a = jnp.where(odd, s, c)
    sin_a = jnp.where(odd, c, s)
    cos_a = jnp.where((quarter == 1) | (quarter == 2), -cos_a, cos_a)
    sin_a = jnp.where((quarter == 2) | (quarter == 3), -sin_a, sin_a)
    return cos_a, sin_a


def own_coefficients(pose, latent):
    lane = lax.broadcasted_iota(jnp.int32, (1, 128), 1)
    n = jnp.full((1, 128), pose, jnp.int32)
    cos_b = 1.0 - (2 * n + 1).astype(jnp.float32) * (1.0 / NROT)
    sin_b = jnp.sqrt(1.0 - cos_b * cos_b)
    cos_a, sin_a = cos_sin(jnp.full((1, 128), lax.rem(pose * 55, 144), jnp.int32))
    cos_g, sin_g = cos_sin(jnp.full((1, 128), lax.rem(pose, 8) * 18, jnp.int32))
    rows = (
        (
            cos_a * cos_b * cos_g - sin_a * sin_g,
            -cos_a * cos_b * sin_g - sin_a * cos_g,
            cos_a * sin_b,
        ),
        (
            sin_a * cos_b * cos_g + cos_a * sin_g,
            -sin_a * cos_b * sin_g + cos_a * cos_g,
            sin_a * sin_b,
        ),
    )
    spread = latent + pltpu.roll(latent, K, 1) + pltpu.roll(latent, 2 * K, 1)
    spread = jnp.where(lane < 3 * K, spread, jnp.where(lane < 3 * K + 3, 1.0, 0.0))
    first = (lane < K) | (lane == 3 * K)
    second = ((lane >= K) & (lane < 2 * K)) | (lane == 3 * K + 1)
    return [spread * jnp.where(first, r[0], jnp.where(second, r[1], r[2])) for r in rows]


def kernel(
    ng,
    ni,
    pose_ref,
    order_ref,
    lat_ref,
    obs_hbm,
    base_hbm,
    amp_hbm,
    wid_hbm,
    modes_hbm,
    res_hbm,
    new_hbm,
    zpad,
    obs,
    rows_in,
    base_in,
    amp,
    wid,
    curve,
    psend,
    params,
    xbuf,
    asend,
    arecv,
    shift,
    weights,
    wmat,
    proj,
    pixels,
    pu0,
    pu1,
    pv0,
    pv1,
    image,
    isend,
    irecv,
    resid,
    rsend,
    whole,
    whole_t,
    grads,
    gown,
    gsend,
    grecv,
    gall,
    gpart,
    mgrad,
    s2,
    newv,
    in_sem,
    out_sem,
    p_sem,
    a_sem,
    i_sem,
    r_sem,
    g_sem,
    s2_sem,
):
    rows = PIX // ng
    pairs = ni * SUB // BLK // 2
    tiles = ni * TILES
    pus, pvs = (pu0, pu1), (pv0, pv1)
    entries = 3 * K * SUB * ni * ng
    gj = lax.axis_index("gauss")
    ib = lax.axis_index("img")

    loads = [
        pltpu.make_async_copy(modes_hbm, rows_in.at[pl.ds(0, 3 * K)], in_sem.at[0]),
        pltpu.make_async_copy(
            base_hbm.at[:, pl.ds(pl.multiple_of(ib * SUB, SUB), SUB)], base_in, in_sem.at[1]
        ),
        pltpu.make_async_copy(amp_hbm, amp, in_sem.at[2]),
        pltpu.make_async_copy(wid_hbm, wid, in_sem.at[3]),
        pltpu.make_async_copy(obs_hbm, obs, in_sem.at[4]),
    ]
    for copy in loads:
        copy.start()

    def partner(axis, n, r):
        me = ib if axis == "img" else gj
        return lax.rem(me + (n // 2 + r if r < n // 2 else n - r), n)

    barrier = pltpu.get_barrier_semaphore()
    for axis, n in (("gauss", ng), ("img", ni)):
        for r in range(1, n):
            pl.semaphore_signal(
                barrier, inc=1, device_id={axis: partner(axis, n, r)}, device_id_type=MESH
            )

    zpad[...] = jnp.zeros_like(zpad)
    zpad[0:4, 0:K] = lat_ref[...]
    chosen = [order_ref[s] for s in range(STEPS)]
    psend[...] = jnp.zeros_like(psend)
    for s in range(STEPS):
        both = own_coefficients(pose_ref[chosen[s]], zpad[pl.ds(chosen[s], 1), :])
        psend[2 * s : 2 * s + 1, :] = both[0]
        psend[2 * s + 1 : 2 * s + 2, :] = both[1]
    params[ib] = psend[...]

    pl.semaphore_wait(barrier, ni + ng - 2)

    def send_all(axis, source, target, sem):
        me, n = (ib, ni) if axis == "img" else (gj, ng)
        for r in range(1, n):
            peer = partner(axis, n, r)
            pltpu.make_async_remote_copy(
                src_ref=source(peer),
                dst_ref=target(me, r),
                send_sem=sem.at[0],
                recv_sem=sem.at[1],
                device_id={axis: peer},
                device_id_type=MESH,
            ).start()

    def wait_for(part, sem):
        pltpu.make_async_copy(part, part, sem).wait()

    send_all("img", lambda peer: psend, lambda me, r: params.at[me], p_sem)

    pixels[...] = lax.broadcasted_iota(jnp.int32, (PIX, 128), 0).astype(jnp.float32)
    loads[0].wait()
    loads[1].wait()
    rows_in[3 * K :, :] = jnp.zeros_like(rows_in[3 * K :, :])
    rows_in[3 * K : 3 * K + 3, :] = base_in[...]
    loads[3].wait()
    w = wid[...]
    inv = 1.0 / (w * w)
    curve[1] = inv
    curve[0] = inv * (-0.5 * math.log2(math.e))

    wait_for(params.at[pl.ds(0, ni - 1)], p_sem.at[1])

    def coefficients(s):
        return jnp.concatenate([params[:, 2 * s, :], params[:, 2 * s + 1, :]], axis=0)

    def project(s):
        got = lax.dot_general(
            coefficients(s)[:, : 3 * K + 8],
            rows_in[...],
            (((1,), (0,)), ((), ())),
            precision=HIGH,
            preferred_element_type=jnp.float32,
        )
        got = got + CENTER
        for t in range(TILES):
            xbuf[t] = got[:, t * 128 : (t + 1) * 128]
        for b in range(ni):
            for uv in range(2):
                asend[s, b, uv] = xbuf[:, uv * ni + b, :]

    project(0)
    send_all("img", lambda peer: asend.at[0, peer], lambda me, r: arecv.at[0, me], a_sem.at[0])
    arecv[0, ib] = asend[0, ib]
    project(1)
    send_all("img", lambda peer: asend.at[1, peer], lambda me, r: arecv.at[1, me], a_sem.at[1])
    arecv[1, ib] = asend[1, ib]
    loads[2].wait()
    wait_for(arecv.at[0, pl.ds(0, ni - 1)], a_sem.at[0, 1])

    halves = []

    for s in range(STEPS):
        if s == 0:
            proj[...] = arecv[0]
        else:
            wait_for(arecv.at[1, pl.ds(0, ni - 1)], a_sem.at[1, 1])
            proj[...] = arecv[1] - halves[0] * shift[...]

        image[...] = jnp.zeros_like(image)

        def profiles(half, j):
            for t in range(BLK // 128):
                g = (2 * j + half) * (BLK // 128) + t
                b, row = g // TILES, g % TILES
                c = curve[0, pl.ds(g, 1), :]
                lanes = slice(t * 128, (t + 1) * 128)
                d = pixels[...] - proj[b, 0, pl.ds(row, 1), :]
                pus[half][j, :, lanes] = jnp.exp2(d * d * c).astype(jnp.bfloat16)
                d = pixels[...] - proj[b, 1, pl.ds(row, 1), :]
                pvs[half][j, :, lanes] = (amp[pl.ds(g, 1), :] * jnp.exp2(d * d * c)).astype(
                    jnp.bfloat16
                )

        def add_image(half, j):
            image[...] += lax.dot_general(
                pus[half][j],
                pvs[half][j],
                (((1,), (1,)), ((), ())),
                preferred_element_type=jnp.float32,
            )

        def render(j, carry):
            add_image(0, j - 1)
            profiles(1, j - 1)
            add_image(1, j - 1)
            profiles(0, j)
            return carry

        profiles(0, 0)
        lax.fori_loop(1, pairs, render, 0)
        add_image(0, pairs - 1)
        profiles(1, pairs - 1)
        add_image(1, pairs - 1)

        for j in range(ng):
            isend[s, j] = image[j * rows : (j + 1) * rows, :].astype(isend.dtype)
        send_all(
            "gauss",
            lambda peer: isend.at[s, peer],
            lambda me, r: irecv.at[s, r - 1],
            i_sem.at[s],
        )
        if s == 0:
            loads[4].wait()
        measured = obs[chosen[s]].astype(jnp.float32)
        total = image[pl.ds(pl.multiple_of(gj * rows, rows), rows), :] - measured
        cross = coefficients(s)[:, : 3 * K]
        other = jnp.concatenate([cross, psend[:, : 3 * K]], axis=0)
        wmat[...] = lax.dot_general(
            other,
            cross,
            (((1,), (1,)), ((), ())),
            precision=HIGH,
            preferred_element_type=jnp.float32,
        )
        for i in range(2 * ni):
            for k in range(i, 2 * ni):
                factor = 1.0 if i == k else 2.0
                weights[i, k] = jnp.broadcast_to(factor * wmat[i : i + 1, k : k + 1], (8, 128))
        if s == 0:
            for i in range(2 * ni):
                for uv in range(2):
                    at = 2 * ni + 2 + uv
                    weights[2 * ni + uv, i] = jnp.broadcast_to(
                        wmat[at : at + 1, i : i + 1], (8, 128)
                    )
        wait_for(irecv.at[s], i_sem.at[s, 1])
        for r in range(ng - 1):
            total = total + irecv[s, r].astype(jnp.float32)
        rsend[s] = total.astype(jnp.bfloat16)
        send_all("gauss", lambda peer: rsend.at[s], lambda me, r: whole.at[s, me], r_sem.at[s])
        whole[s, gj] = rsend[s]
        if s == STEPS - 1:
            resid[...] = total
            pltpu.make_async_copy(resid, res_hbm, out_sem.at[0]).start()
        wait_for(whole.at[s, pl.ds(0, ng - 1)], r_sem.at[s, 1])
        whole_t[0] = whole[s].reshape(PIX, PIX)
        whole_t[1] = whole_t[0].T

        def backward(j, carry):
            for half in range(2):
                sides = ((0, pus, whole_t[0], pvs), (1, pvs, whole_t[1], pus))
                for uv, own, matrix, other in sides:
                    weighted = jnp.dot(matrix, other[half][j], preferred_element_type=jnp.float32)
                    for t in range(BLK // 128):
                        g = (2 * j + half) * (BLK // 128) + t
                        b, row = g // TILES, g % TILES
                        lanes = slice(t * 128, (t + 1) * 128)
                        d = pixels[...] - proj[b, uv, pl.ds(row, 1), :]
                        total = own[half][j, :, lanes].astype(jnp.float32) * d * weighted[:, lanes]
                        gown[pl.ds(uv * tiles + g, 1), :] = curve[1, pl.ds(g, 1), :] * jnp.sum(
                            total, axis=0, keepdims=True
                        )
            return carry

        lax.fori_loop(0, pairs, backward, 0)

        gsend[s] = gown[...].astype(jnp.bfloat16)
        send_all("img", lambda peer: gsend.at[s], lambda me, r: grecv.at[s, me], g_sem.at[s])
        grecv[s, ib] = gsend[s]
        wait_for(grecv.at[s, pl.ds(0, ni - 1)], g_sem.at[s, 1])
        gall[...] = grecv[s].astype(jnp.float32)

        def gradient(i):
            return gall[i % ni, (i // ni) * tiles : (i // ni + 1) * tiles, :]

        squares = jnp.zeros((8, 128), jnp.float32)
        for i in range(2 * ni):
            gi = gradient(i)
            for k in range(i, 2 * ni):
                product = (gi * gradient(k)).reshape(tiles // 8, 8, 128)
                squares = squares + weights[i, k] * jnp.sum(product, axis=0)
        s2[s, gj] = squares
        send_all("gauss", lambda peer: s2.at[s, gj], lambda me, r: s2.at[s, me], s2_sem.at[s])
        if s == 0:
            for uv in range(2):
                moved = jnp.zeros((ni, TILES, 128), jnp.float32)
                for i in range(2 * ni):
                    moved = moved + weights[2 * ni + uv, i] * gradient(i).reshape(ni, TILES, 128)
                shift[:, uv] = moved
        for b in range(ni):
            for uv in range(2):
                first = pl.multiple_of(uv * tiles + ib * TILES, TILES)
                gpart[b, uv] = gall[b, pl.ds(first, TILES), :]
        for uv in range(2):
            for t in range(TILES):
                grads[uv * ni : (uv + 1) * ni, t * 128 : (t + 1) * 128] = gpart[:, uv, t, :]
        mgrad[s] = lax.dot_general(
            coefficients(s)[:, : 3 * K],
            grads[...],
            (((0,), (0,)), ((), ())),
            precision=HIGH,
            preferred_element_type=jnp.float32,
        )
        if s == 1:
            newv[...] = rows_in[: 3 * K, :] - halves[0] * mgrad[0]
        wait_for(s2.at[s, pl.ds(0, ng - 1)], s2_sem.at[s, 1])
        sums = jnp.sum(s2[s], axis=0)
        sums = jnp.sum(jnp.sum(sums, axis=0, keepdims=True), axis=1, keepdims=True)
        halves.append(step_size / jnp.sqrt(sums * (1.0 / entries) + tiny_eps))

    newv[...] = newv[...] - halves[1] * mgrad[1]
    done = pltpu.make_async_copy(newv, new_hbm, out_sem.at[1])
    done.start()

    wait_for(params.at[pl.ds(0, ni - 1)], p_sem.at[0])
    for s in range(STEPS):
        wait_for(arecv.at[s, pl.ds(0, ni - 1)], a_sem.at[s, 0])
        wait_for(irecv.at[s], i_sem.at[s, 0])
        wait_for(whole.at[s, pl.ds(0, ng - 1)], r_sem.at[s, 0])
        wait_for(grecv.at[s, pl.ds(0, ni - 1)], g_sem.at[s, 0])
        wait_for(s2.at[s, pl.ds(0, ng - 1)], s2_sem.at[s, 0])
    pltpu.make_async_copy(resid, res_hbm, out_sem.at[0]).wait()
    done.wait()


def body(
    observed, pose_index, batch_order, latents, base_positions, amplitudes, widths, deform_modes
):
    ng, ni = lax.axis_size("gauss"), lax.axis_size("img")
    rows = PIX // ng
    count = ni * SUB
    pairs = count // BLK // 2
    f32, b16 = jnp.float32, jnp.bfloat16
    vmem, hbm, smem = (
        pl.BlockSpec(memory_space=m) for m in (pltpu.VMEM, pl.ANY, pltpu.SMEM)
    )
    dma = pltpu.SemaphoreType.DMA
    final, new = pl.pallas_call(
        functools.partial(kernel, ng, ni),
        out_shape=(
            jax.ShapeDtypeStruct((rows, PIX), f32),
            jax.ShapeDtypeStruct((3 * K, SUB), f32),
        ),
        in_specs=[smem, smem, vmem, hbm, hbm, hbm, hbm, hbm],
        out_specs=(hbm, hbm),
        scratch_shapes=[
            pltpu.VMEM((8, 128), f32),
            pltpu.VMEM((4, rows, PIX), b16),
            pltpu.VMEM((3 * K + 8, SUB), f32),
            pltpu.VMEM((3, SUB), f32),
            pltpu.VMEM((count // 128, 128), f32),
            pltpu.VMEM((count // 128, 128), f32),
            pltpu.VMEM((2, count // 128, 128), f32),
            pltpu.VMEM((8, 128), f32),
            pltpu.VMEM((ni, 8, 128), f32),
            pltpu.VMEM((TILES, 2 * ni, 128), f32),
            pltpu.VMEM((STEPS, ni, 2, TILES, 128), f32),
            pltpu.VMEM((STEPS, ni, 2, TILES, 128), f32),
            pltpu.VMEM((ni, 2, TILES, 128), f32),
            pltpu.VMEM((2 * ni + 2, 2 * ni, 8, 128), f32),
            pltpu.VMEM((2 * ni + 8, 2 * ni), f32),
            pltpu.VMEM((ni, 2, TILES, 128), f32),
            pltpu.VMEM((PIX, 128), f32),
            pltpu.VMEM((pairs, PIX, BLK), b16),
            pltpu.VMEM((pairs, PIX, BLK), b16),
            pltpu.VMEM((pairs, PIX, BLK), b16),
            pltpu.VMEM((pairs, PIX, BLK), b16),
            pltpu.VMEM((PIX, PIX), f32),
            pltpu.VMEM((STEPS, ng, rows, PIX), b16),
            pltpu.VMEM((STEPS, ng - 1, rows, PIX), b16),
            pltpu.VMEM((rows, PIX), f32),
            pltpu.VMEM((STEPS, rows, PIX), b16),
            pltpu.VMEM((STEPS, ng, rows, PIX), b16),
            pltpu.VMEM((2, PIX, PIX), b16),
            pltpu.VMEM((2 * ni, SUB), f32),
            pltpu.VMEM((2 * count // 128, 128), f32),
            pltpu.VMEM((STEPS, 2 * count // 128, 128), b16),
            pltpu.VMEM((STEPS, ni, 2 * count // 128, 128), b16),
            pltpu.VMEM((ni, 2 * count // 128, 128), f32),
            pltpu.VMEM((ni, 2, TILES, 128), f32),
            pltpu.VMEM((STEPS, 3 * K, SUB), f32),
            pltpu.VMEM((STEPS, ng, 8, 128), f32),
            pltpu.VMEM((3 * K, SUB), f32),
            dma((5,)),
            dma((2,)),
            dma((2,)),
            dma((STEPS, 2)),
            dma((STEPS, 2)),
            dma((STEPS, 2)),
            dma((STEPS, 2)),
            dma((STEPS, 2)),
        ],
        compiler_params=pltpu.CompilerParams(
            collective_id=0, has_side_effects=True, vmem_limit_bytes=60 * 2**20
        ),
    )(
        pose_index,
        batch_order,
        latents,
        observed,
        base_positions,
        amplitudes.reshape(count // 128, 128),
        widths.reshape(count // 128, 128),
        deform_modes.transpose(1, 0, 2).reshape(3 * K, SUB),
    )
    return final[None], new.reshape(3, K, SUB).transpose(1, 0, 2)


def solution(mesh):
    return jax.shard_map(
        body,
        mesh=mesh,
        in_specs=(
            P("img", "gauss", None),
            P("img"),
            P("img"),
            P("img", None),
            P(None, "gauss"),
            P("gauss"),
            P("gauss"),
            P(None, None, ("gauss", "img")),
        ),
        out_specs=(P("img", "gauss", None), P(None, None, ("gauss", "img"))),
        check_vma=False,
    )
```

```python
import functools
import math

import jax
import jax.numpy as jnp
from jax import lax
from jax.experimental import pallas as pl
from jax.experimental.pallas import tpu as pltpu
from jax.sharding import PartitionSpec as P

PIX = 256
K = 16
NROT = 4096
STEPS = 2
SUB = 1024
TILES = SUB // 128
CHUNK = 2048
SUBS = CHUNK // SUB
CTILES = CHUNK // 128
BLK = 512
CENTER = (PIX - 1) * 0.5

step_size = 0.5
tiny_eps = 1e-06
MESH = pl.DeviceIdType.MESH
HIGH = lax.Precision.HIGHEST


def cos_sin(units):
    quarter = (
        (units >= 18).astype(jnp.int32)
        + (units >= 54).astype(jnp.int32)
        + (units >= 90).astype(jnp.int32)
        + (units >= 126).astype(jnp.int32)
    )
    x = (units - 36 * quarter).astype(jnp.float32) * (2.0 * math.pi / 144.0)
    y = x * x
    s = x * (1.0 + y * (-1.0 / 6 + y * (1.0 / 120 + y * (-1.0 / 5040 + y * (1.0 / 362880)))))
    c = 1.0 + y * (
        -0.5 + y * (1.0 / 24 + y * (-1.0 / 720 + y * (1.0 / 40320 - y * (1.0 / 3628800))))
    )
    odd = (quarter == 1) | (quarter == 3)
    cos_a = jnp.where(odd, s, c)
    sin_a = jnp.where(odd, c, s)
    cos_a = jnp.where((quarter == 1) | (quarter == 2), -cos_a, cos_a)
    sin_a = jnp.where((quarter == 2) | (quarter == 3), -sin_a, sin_a)
    return cos_a, sin_a


def own_coefficients(pose, latent):
    lane = lax.broadcasted_iota(jnp.int32, (1, 128), 1)
    n = jnp.full((1, 128), pose, jnp.int32)
    cos_b = 1.0 - (2 * n + 1).astype(jnp.float32) * (1.0 / NROT)
    sin_b = jnp.sqrt(1.0 - cos_b * cos_b)
    cos_a, sin_a = cos_sin(jnp.full((1, 128), lax.rem(pose * 55, 144), jnp.int32))
    cos_g, sin_g = cos_sin(jnp.full((1, 128), lax.rem(pose, 8) * 18, jnp.int32))
    rows = (
        (
            cos_a * cos_b * cos_g - sin_a * sin_g,
            -cos_a * cos_b * sin_g - sin_a * cos_g,
            cos_a * sin_b,
        ),
        (
            sin_a * cos_b * cos_g + cos_a * sin_g,
            -sin_a * cos_b * sin_g + cos_a * cos_g,
            sin_a * sin_b,
        ),
    )
    spread = latent + pltpu.roll(latent, K, 1) + pltpu.roll(latent, 2 * K, 1)
    spread = jnp.where(lane < 3 * K, spread, jnp.where(lane < 3 * K + 3, 1.0, 0.0))
    first = (lane < K) | (lane == 3 * K)
    second = ((lane >= K) & (lane < 2 * K)) | (lane == 3 * K + 1)
    return [spread * jnp.where(first, r[0], jnp.where(second, r[1], r[2])) for r in rows]


def kernel(
    ng,
    ni,
    pose_ref,
    order_ref,
    lat_ref,
    obs_hbm,
    base_hbm,
    amp_hbm,
    wid_hbm,
    modes_hbm,
    res_hbm,
    new_hbm,
    zpad,
    obs,
    rows_in,
    base_in,
    amp,
    wid,
    curve,
    psend,
    params,
    xbuf,
    asend,
    arecv,
    shift,
    weights,
    wmat,
    proj,
    pixels,
    pu,
    pv,
    image,
    isend,
    irecv,
    resid,
    rsend,
    whole,
    whole_t,
    grads,
    gown,
    gsend,
    grecv,
    gall,
    gpart,
    mgrad,
    s2,
    newv,
    in_sem,
    out_sem,
    p_sem,
    a_sem,
    i_sem,
    r_sem,
    g_sem,
    s2_sem,
):
    rows = PIX // ng
    chunks = ni * SUB // CHUNK
    entries = 3 * K * SUB * ni * ng
    gj = lax.axis_index("gauss")
    ib = lax.axis_index("img")

    loads = [
        pltpu.make_async_copy(modes_hbm, rows_in.at[pl.ds(0, 3 * K)], in_sem.at[0]),
        pltpu.make_async_copy(
            base_hbm.at[:, pl.ds(pl.multiple_of(ib * SUB, SUB), SUB)], base_in, in_sem.at[1]
        ),
        pltpu.make_async_copy(amp_hbm, amp, in_sem.at[2]),
        pltpu.make_async_copy(wid_hbm, wid, in_sem.at[3]),
        pltpu.make_async_copy(obs_hbm, obs, in_sem.at[4]),
    ]
    for copy in loads:
        copy.start()

    def partner(axis, n, r):
        me = ib if axis == "img" else gj
        return lax.rem(me + (n // 2 + r if r < n // 2 else n - r), n)

    barrier = pltpu.get_barrier_semaphore()
    for axis, n in (("gauss", ng), ("img", ni)):
        for r in range(1, n):
            pl.semaphore_signal(
                barrier, inc=1, device_id={axis: partner(axis, n, r)}, device_id_type=MESH
            )

    zpad[...] = jnp.zeros_like(zpad)
    zpad[0:4, 0:K] = lat_ref[...]
    chosen = [order_ref[s] for s in range(STEPS)]
    psend[...] = jnp.zeros_like(psend)
    for s in range(STEPS):
        both = own_coefficients(pose_ref[chosen[s]], zpad[pl.ds(chosen[s], 1), :])
        psend[2 * s : 2 * s + 1, :] = both[0]
        psend[2 * s + 1 : 2 * s + 2, :] = both[1]
    params[ib] = psend[...]

    pl.semaphore_wait(barrier, ni + ng - 2)

    def send_all(axis, source, target, sem):
        me, n = (ib, ni) if axis == "img" else (gj, ng)
        for r in range(1, n):
            peer = partner(axis, n, r)
            pltpu.make_async_remote_copy(
                src_ref=source(peer),
                dst_ref=target(me, r),
                send_sem=sem.at[0],
                recv_sem=sem.at[1],
                device_id={axis: peer},
                device_id_type=MESH,
            ).start()

    def wait_for(part, sem):
        pltpu.make_async_copy(part, part, sem).wait()

    send_all("img", lambda peer: psend, lambda me, r: params.at[me], p_sem)

    pixels[...] = lax.broadcasted_iota(jnp.int32, (PIX, 128), 0).astype(jnp.float32)
    loads[0].wait()
    loads[1].wait()
    rows_in[3 * K :, :] = jnp.zeros_like(rows_in[3 * K :, :])
    rows_in[3 * K : 3 * K + 3, :] = base_in[...]
    loads[3].wait()
    w = wid[...]
    inv = 1.0 / (w * w)
    curve[1] = inv
    curve[0] = inv * (-0.5 * math.log2(math.e))

    wait_for(params.at[pl.ds(0, ni - 1)], p_sem.at[1])

    def coefficients(s):
        return jnp.concatenate([params[:, 2 * s, :], params[:, 2 * s + 1, :]], axis=0)

    def project(s):
        got = lax.dot_general(
            coefficients(s)[:, : 3 * K + 8],
            rows_in[...],
            (((1,), (0,)), ((), ())),
            precision=HIGH,
            preferred_element_type=jnp.float32,
        )
        got = got + CENTER
        for t in range(TILES):
            xbuf[t] = got[:, t * 128 : (t + 1) * 128]
        for b in range(ni):
            for uv in range(2):
                asend[s, b, uv] = xbuf[:, uv * ni + b, :]

    project(0)
    send_all("img", lambda peer: asend.at[0, peer], lambda me, r: arecv.at[0, me], a_sem.at[0])
    arecv[0, ib] = asend[0, ib]
    project(1)
    send_all("img", lambda peer: asend.at[1, peer], lambda me, r: arecv.at[1, me], a_sem.at[1])
    arecv[1, ib] = asend[1, ib]
    loads[2].wait()
    halves = []

    for s in range(STEPS):
        def profiles(b):
            for t in range(TILES):
                g = b * TILES + t
                c = curve[0, pl.ds(g, 1), :]
                first = pl.multiple_of((b % SUBS) * SUB + t * 128, 128)
                d = pixels[...] - proj[b, 0, t : t + 1, :]
                pu[b // SUBS, :, pl.ds(first, 128)] = jnp.exp2(d * d * c).astype(jnp.bfloat16)
                d = pixels[...] - proj[b, 1, t : t + 1, :]
                pv[b // SUBS, :, pl.ds(first, 128)] = (
                    amp[pl.ds(g, 1), :] * jnp.exp2(d * d * c)
                ).astype(jnp.bfloat16)

        if s == 0:
            proj[ib] = arecv[0, ib]
            profiles(ib)
            wait_for(arecv.at[0, pl.ds(0, ni - 1)], a_sem.at[0, 1])
            proj[...] = arecv[0]
        else:
            wait_for(arecv.at[1, pl.ds(0, ni - 1)], a_sem.at[1, 1])
            proj[...] = arecv[1] - halves[0] * shift[...]

        def render(i, carry):
            profiles(lax.rem(ib + i, ni))
            return carry

        lax.fori_loop(1 if s == 0 else 0, ni, render, 0)

        image[...] = jnp.zeros_like(image)
        together = 2 if chunks % 2 == 0 else 1

        def add_image(i, carry):
            terms = [
                lax.dot_general(
                    pu[i * together + k],
                    pv[i * together + k],
                    (((1,), (1,)), ((), ())),
                    preferred_element_type=jnp.float32,
                )
                for k in range(together)
            ]
            image[...] += sum(terms)
            return carry

        lax.fori_loop(0, chunks // together, add_image, 0)

        for j in range(ng):
            isend[s, j] = image[j * rows : (j + 1) * rows, :].astype(isend.dtype)
        send_all(
            "gauss",
            lambda peer: isend.at[s, peer],
            lambda me, r: irecv.at[s, r - 1],
            i_sem.at[s],
        )
        if s == 0:
            loads[4].wait()
        measured = obs[chosen[s]].astype(jnp.float32)
        total = image[pl.ds(pl.multiple_of(gj * rows, rows), rows), :] - measured
        cross = coefficients(s)[:, : 3 * K]
        other = jnp.concatenate([cross, psend[:, : 3 * K]], axis=0)
        wmat[...] = lax.dot_general(
            other,
            cross,
            (((1,), (1,)), ((), ())),
            precision=HIGH,
            preferred_element_type=jnp.float32,
        )
        for i in range(2 * ni):
            for k in range(i, 2 * ni):
                factor = 1.0 if i == k else 2.0
                weights[i, k] = jnp.broadcast_to(factor * wmat[i : i + 1, k : k + 1], (8, 128))
        if s == 0:
            for i in range(2 * ni):
                for uv in range(2):
                    at = 2 * ni + 2 + uv
                    weights[2 * ni + uv, i] = jnp.broadcast_to(
                        wmat[at : at + 1, i : i + 1], (8, 128)
                    )
        wait_for(irecv.at[s], i_sem.at[s, 1])
        for r in range(ng - 1):
            total = total + irecv[s, r].astype(jnp.float32)
        rsend[s] = total.astype(jnp.bfloat16)
        send_all("gauss", lambda peer: rsend.at[s], lambda me, r: whole.at[s, me], r_sem.at[s])
        whole[s, gj] = rsend[s]
        if s == STEPS - 1:
            resid[...] = total
            pltpu.make_async_copy(resid, res_hbm, out_sem.at[0]).start()
        wait_for(whole.at[s, pl.ds(0, ng - 1)], r_sem.at[s, 1])
        whole_t[0] = whole[s].reshape(PIX, PIX)
        whole_t[1] = whole_t[0].T

        def backward(c, carry):
            def part(k, carry):
                for half in range(2):
                    at = (2 * k + half) * BLK
                    cols = pl.ds(pl.multiple_of(at, BLK), BLK)
                    for uv, own, matrix, other in ((0, pu, whole_t[0], pv), (1, pv, whole_t[1], pu)):
                        weighted = jnp.dot(
                            matrix, other[c, :, cols], preferred_element_type=jnp.float32
                        )
                        for t in range(BLK // 128):
                            tile = (2 * k + half) * (BLK // 128) + t
                            g = c * CTILES + tile
                            col = pl.ds(pl.multiple_of(at + t * 128, 128), 128)
                            d = pixels[...] - proj[g // TILES, uv, pl.ds(g % TILES, 1), :]
                            total = (
                                own[c, :, col].astype(jnp.float32)
                                * d
                                * weighted[:, t * 128 : (t + 1) * 128]
                            )
                            gown[pl.ds(uv * CTILES + tile, 1), :] = curve[
                                1, pl.ds(g, 1), :
                            ] * jnp.sum(total, axis=0, keepdims=True)
                return carry

            lax.fori_loop(0, CHUNK // (2 * BLK), part, 0)
            gsend[s, c] = gown[...].astype(jnp.bfloat16)
            send_all(
                "img",
                lambda peer: gsend.at[s, c],
                lambda me, r: grecv.at[s, c, me],
                g_sem.at[s, c],
            )
            grecv[s, c, ib] = gsend[s, c]
            return carry

        lax.fori_loop(0, chunks, backward, 0)

        def gradient(c, i):
            return gall[c, i % ni, (i // ni) * CTILES : (i // ni + 1) * CTILES, :]

        def add_squares(c, squares):
            wait_for(grecv.at[s, c, pl.ds(0, ni - 1)], g_sem.at[s, c, 1])
            gall[c] = grecv[s, c].astype(jnp.float32)
            for i in range(2 * ni):
                gi = gradient(c, i)
                for k in range(i, 2 * ni):
                    product = gi * gradient(c, k)
                    squares = squares + weights[i, k] * jnp.sum(
                        product.reshape(CTILES // 8, 8, 128), axis=0
                    )
            return squares

        squares = lax.fori_loop(0, chunks, add_squares, jnp.zeros((8, 128), jnp.float32))
        s2[s, gj] = jnp.sum(squares, axis=0, keepdims=True)
        send_all("gauss", lambda peer: s2.at[s, gj], lambda me, r: s2.at[s, me], s2_sem.at[s])
        if s == 0:

            def move(c, carry):
                for uv in range(2):
                    moved = jnp.zeros((SUBS, TILES, 128), jnp.float32)
                    for i in range(2 * ni):
                        moved = moved + weights[2 * ni + uv, i] * gradient(c, i).reshape(
                            SUBS, TILES, 128
                        )
                    shift[pl.ds(c * SUBS, SUBS), uv] = moved
                return carry

            lax.fori_loop(0, chunks, move, 0)
        for b in range(ni):
            for uv in range(2):
                first = pl.multiple_of(uv * CTILES + (ib % SUBS) * TILES, TILES)
                gpart[b, uv] = gall[ib // SUBS, b, pl.ds(first, TILES), :]
        for uv in range(2):
            for t in range(TILES):
                grads[uv * ni : (uv + 1) * ni, t * 128 : (t + 1) * 128] = gpart[:, uv, t, :]
        mgrad[s] = lax.dot_general(
            coefficients(s)[:, : 3 * K],
            grads[...],
            (((0,), (0,)), ((), ())),
            precision=HIGH,
            preferred_element_type=jnp.float32,
        )
        if s == 1:
            newv[...] = rows_in[: 3 * K, :] - halves[0] * mgrad[0]
        wait_for(s2.at[s, pl.ds(0, ng - 1)], s2_sem.at[s, 1])
        sums = jnp.sum(s2[s], axis=0)
        sums = jnp.sum(jnp.sum(sums, axis=0, keepdims=True), axis=1, keepdims=True)
        halves.append(step_size / jnp.sqrt(sums * (1.0 / entries) + tiny_eps))

    newv[...] = newv[...] - halves[1] * mgrad[1]
    done = pltpu.make_async_copy(newv, new_hbm, out_sem.at[1])
    done.start()

    wait_for(params.at[pl.ds(0, ni - 1)], p_sem.at[0])
    for s in range(STEPS):
        wait_for(arecv.at[s, pl.ds(0, ni - 1)], a_sem.at[s, 0])
        wait_for(irecv.at[s], i_sem.at[s, 0])
        wait_for(whole.at[s, pl.ds(0, ng - 1)], r_sem.at[s, 0])
        for c in range(chunks):
            wait_for(grecv.at[s, c, pl.ds(0, ni - 1)], g_sem.at[s, c, 0])
        wait_for(s2.at[s, pl.ds(0, ng - 1)], s2_sem.at[s, 0])
    pltpu.make_async_copy(resid, res_hbm, out_sem.at[0]).wait()
    done.wait()


def body(
    observed, pose_index, batch_order, latents, base_positions, amplitudes, widths, deform_modes
):
    ng, ni = lax.axis_size("gauss"), lax.axis_size("img")
    rows = PIX // ng
    count = ni * SUB
    chunks = count // CHUNK
    f32, b16 = jnp.float32, jnp.bfloat16
    vmem, hbm, smem = (
        pl.BlockSpec(memory_space=m) for m in (pltpu.VMEM, pl.ANY, pltpu.SMEM)
    )
    dma = pltpu.SemaphoreType.DMA
    final, new = pl.pallas_call(
        functools.partial(kernel, ng, ni),
        out_shape=(
            jax.ShapeDtypeStruct((rows, PIX), f32),
            jax.ShapeDtypeStruct((3 * K, SUB), f32),
        ),
        in_specs=[smem, smem, vmem, hbm, hbm, hbm, hbm, hbm],
        out_specs=(hbm, hbm),
        scratch_shapes=[
            pltpu.VMEM((8, 128), f32),
            pltpu.VMEM((4, rows, PIX), b16),
            pltpu.VMEM((3 * K + 8, SUB), f32),
            pltpu.VMEM((3, SUB), f32),
            pltpu.VMEM((count // 128, 128), f32),
            pltpu.VMEM((count // 128, 128), f32),
            pltpu.VMEM((2, count // 128, 128), f32),
            pltpu.VMEM((8, 128), f32),
            pltpu.VMEM((ni, 8, 128), f32),
            pltpu.VMEM((TILES, 2 * ni, 128), f32),
            pltpu.VMEM((STEPS, ni, 2, TILES, 128), f32),
            pltpu.VMEM((STEPS, ni, 2, TILES, 128), f32),
            pltpu.VMEM((ni, 2, TILES, 128), f32),
            pltpu.VMEM((2 * ni + 2, 2 * ni, 8, 128), f32),
            pltpu.VMEM((2 * ni + 8, 2 * ni), f32),
            pltpu.VMEM((ni, 2, TILES, 128), f32),
            pltpu.VMEM((PIX, 128), f32),
            pltpu.VMEM((chunks, PIX, CHUNK), b16),
            pltpu.VMEM((chunks, PIX, CHUNK), b16),
            pltpu.VMEM((PIX, PIX), f32),
            pltpu.VMEM((STEPS, ng, rows, PIX), b16),
            pltpu.VMEM((STEPS, ng - 1, rows, PIX), b16),
            pltpu.VMEM((rows, PIX), f32),
            pltpu.VMEM((STEPS, rows, PIX), b16),
            pltpu.VMEM((STEPS, ng, rows, PIX), b16),
            pltpu.VMEM((2, PIX, PIX), b16),
            pltpu.VMEM((2 * ni, SUB), f32),
            pltpu.VMEM((2 * CTILES, 128), f32),
            pltpu.VMEM((STEPS, chunks, 2 * CTILES, 128), b16),
            pltpu.VMEM((STEPS, chunks, ni, 2 * CTILES, 128), b16),
            pltpu.VMEM((chunks, ni, 2 * CTILES, 128), f32),
            pltpu.VMEM((ni, 2, TILES, 128), f32),
            pltpu.VMEM((STEPS, 3 * K, SUB), f32),
            pltpu.VMEM((STEPS, ng, 1, 128), f32),
            pltpu.VMEM((3 * K, SUB), f32),
            dma((5,)),
            dma((2,)),
            dma((2,)),
            dma((STEPS, 2)),
            dma((STEPS, 2)),
            dma((STEPS, 2)),
            dma((STEPS, chunks, 2)),
            dma((STEPS, 2)),
        ],
        compiler_params=pltpu.CompilerParams(
            collective_id=0, has_side_effects=True, vmem_limit_bytes=60 * 2**20
        ),
    )(
        pose_index,
        batch_order,
        latents,
        observed,
        base_positions,
        amplitudes.reshape(count // 128, 128),
        widths.reshape(count // 128, 128),
        deform_modes.transpose(1, 0, 2).reshape(3 * K, SUB),
    )
    return final[None], new.reshape(3, K, SUB).transpose(1, 0, 2)


def solution(mesh):
    return jax.shard_map(
        body,
        mesh=mesh,
        in_specs=(
            P("img", "gauss", None),
            P("img"),
            P("img"),
            P("img", None),
            P(None, "gauss"),
            P("gauss"),
            P("gauss"),
            P(None, None, ("gauss", "img")),
        ),
        out_specs=(P("img", "gauss", None), P(None, None, ("gauss", "img"))),
        check_vma=False,
    )
```

```python
import functools
import math

import jax
import jax.numpy as jnp
from jax import lax
from jax.experimental import pallas as pl
from jax.experimental.pallas import tpu as pltpu
from jax.sharding import PartitionSpec as P

PIX = 256
K = 16
NROT = 4096
STEPS = 2
SUB = 1024
TILES = SUB // 128
CHUNK = 2048
SUBS = CHUNK // SUB
CTILES = CHUNK // 128
BLK = 1024
CENTER = (PIX - 1) * 0.5

step_size = 0.5
tiny_eps = 1e-06
MESH = pl.DeviceIdType.MESH
HIGH = lax.Precision.HIGHEST


def cos_sin(units):
    quarter = (
        (units >= 18).astype(jnp.int32)
        + (units >= 54).astype(jnp.int32)
        + (units >= 90).astype(jnp.int32)
        + (units >= 126).astype(jnp.int32)
    )
    x = (units - 36 * quarter).astype(jnp.float32) * (2.0 * math.pi / 144.0)
    y = x * x
    s = x * (1.0 + y * (-1.0 / 6 + y * (1.0 / 120 + y * (-1.0 / 5040 + y * (1.0 / 362880)))))
    c = 1.0 + y * (
        -0.5 + y * (1.0 / 24 + y * (-1.0 / 720 + y * (1.0 / 40320 - y * (1.0 / 3628800))))
    )
    odd = (quarter == 1) | (quarter == 3)
    cos_a = jnp.where(odd, s, c)
    sin_a = jnp.where(odd, c, s)
    cos_a = jnp.where((quarter == 1) | (quarter == 2), -cos_a, cos_a)
    sin_a = jnp.where((quarter == 2) | (quarter == 3), -sin_a, sin_a)
    return cos_a, sin_a


def own_coefficients(pose, latent):
    lane = lax.broadcasted_iota(jnp.int32, (1, 128), 1)
    n = jnp.full((1, 128), pose, jnp.int32)
    cos_b = 1.0 - (2 * n + 1).astype(jnp.float32) * (1.0 / NROT)
    sin_b = jnp.sqrt(1.0 - cos_b * cos_b)
    cos_a, sin_a = cos_sin(jnp.full((1, 128), lax.rem(pose * 55, 144), jnp.int32))
    cos_g, sin_g = cos_sin(jnp.full((1, 128), lax.rem(pose, 8) * 18, jnp.int32))
    rows = (
        (
            cos_a * cos_b * cos_g - sin_a * sin_g,
            -cos_a * cos_b * sin_g - sin_a * cos_g,
            cos_a * sin_b,
        ),
        (
            sin_a * cos_b * cos_g + cos_a * sin_g,
            -sin_a * cos_b * sin_g + cos_a * cos_g,
            sin_a * sin_b,
        ),
    )
    spread = latent + pltpu.roll(latent, K, 1) + pltpu.roll(latent, 2 * K, 1)
    spread = jnp.where(lane < 3 * K, spread, jnp.where(lane < 3 * K + 3, 1.0, 0.0))
    first = (lane < K) | (lane == 3 * K)
    second = ((lane >= K) & (lane < 2 * K)) | (lane == 3 * K + 1)
    return [spread * jnp.where(first, r[0], jnp.where(second, r[1], r[2])) for r in rows]


def kernel(
    ng,
    ni,
    pose_hbm,
    order_hbm,
    lat_hbm,
    obs_hbm,
    base_hbm,
    amp_hbm,
    wid_hbm,
    modes_hbm,
    final,
    newv,
    pose_ref,
    order_ref,
    lat_ref,
    zpad,
    obs,
    rows_in,
    base_in,
    amp,
    wid,
    curve,
    psend,
    params,
    xbuf,
    asend,
    arecv,
    shift,
    weights,
    wmat,
    proj,
    pixels,
    pu,
    pv,
    slope_u,
    slope_v,
    image,
    isend,
    irecv,
    rsend,
    whole,
    whole_t,
    grads,
    gown,
    gsend,
    grecv,
    gall,
    gpart,
    mgrad,
    s2,
    in_sem,
    p_sem,
    a_sem,
    i_sem,
    r_sem,
    g_sem,
    s2_sem,
):
    rows = PIX // ng
    chunks = ni * SUB // CHUNK
    entries = 3 * K * SUB * ni * ng
    gj = lax.axis_index("gauss")
    ib = lax.axis_index("img")

    def partner(axis, n, r):
        me = ib if axis == "img" else gj
        return lax.rem(me + (n // 2 + r if r < n // 2 else n - r), n)

    barrier = pltpu.get_barrier_semaphore()
    for axis, n in (("gauss", ng), ("img", ni)):
        for r in range(1, n):
            pl.semaphore_signal(
                barrier, inc=1, device_id={axis: partner(axis, n, r)}, device_id_type=MESH
            )

    loads = [
        pltpu.make_async_copy(pose_hbm, pose_ref, in_sem.at[5]),
        pltpu.make_async_copy(order_hbm, order_ref, in_sem.at[6]),
        pltpu.make_async_copy(lat_hbm, lat_ref, in_sem.at[7]),
        pltpu.make_async_copy(modes_hbm, rows_in.at[pl.ds(0, 3 * K)], in_sem.at[0]),
        pltpu.make_async_copy(
            base_hbm.at[:, pl.ds(pl.multiple_of(ib * SUB, SUB), SUB)], base_in, in_sem.at[1]
        ),
        pltpu.make_async_copy(amp_hbm, amp, in_sem.at[2]),
        pltpu.make_async_copy(wid_hbm, wid, in_sem.at[3]),
        pltpu.make_async_copy(obs_hbm, obs, in_sem.at[4]),
    ]
    for copy in loads:
        copy.start()

    for copy in loads[:3]:
        copy.wait()
    del loads[:3]
    zpad[...] = jnp.zeros_like(zpad)
    zpad[0:4, 0:K] = lat_ref[...]
    chosen = [order_ref[s] for s in range(STEPS)]
    psend[...] = jnp.zeros_like(psend)
    for s in range(STEPS):
        both = own_coefficients(pose_ref[chosen[s]], zpad[pl.ds(chosen[s], 1), :])
        psend[2 * s : 2 * s + 1, :] = both[0]
        psend[2 * s + 1 : 2 * s + 2, :] = both[1]
    params[ib] = psend[...]

    pl.semaphore_wait(barrier, ni + ng - 2)

    def send_all(axis, source, target, sem):
        me, n = (ib, ni) if axis == "img" else (gj, ng)
        for r in range(1, n):
            peer = partner(axis, n, r)
            pltpu.make_async_remote_copy(
                src_ref=source(peer),
                dst_ref=target(me, r),
                send_sem=sem.at[0],
                recv_sem=sem.at[1],
                device_id={axis: peer},
                device_id_type=MESH,
            ).start()

    def wait_for(part, sem):
        pltpu.make_async_copy(part, part, sem).wait()

    send_all("img", lambda peer: psend, lambda me, r: params.at[me], p_sem)

    pixels[...] = lax.broadcasted_iota(jnp.int32, (PIX, 128), 0).astype(jnp.float32)
    loads[0].wait()
    loads[1].wait()
    rows_in[3 * K :, :] = jnp.zeros_like(rows_in[3 * K :, :])
    rows_in[3 * K : 3 * K + 3, :] = base_in[...]
    loads[3].wait()
    w = wid[...]
    inv = 1.0 / (w * w)
    curve[1] = inv
    curve[0] = inv * (-0.5 * math.log2(math.e))

    wait_for(params.at[pl.ds(0, ni - 1)], p_sem.at[1])

    def coefficients(s):
        return jnp.concatenate([params[:, 2 * s, :], params[:, 2 * s + 1, :]], axis=0)

    def project(s):
        got = lax.dot_general(
            coefficients(s)[:, : 3 * K + 8],
            rows_in[...],
            (((1,), (0,)), ((), ())),
            precision=HIGH,
            preferred_element_type=jnp.float32,
        )
        got = got + CENTER
        for t in range(TILES):
            xbuf[t] = got[:, t * 128 : (t + 1) * 128]
        for b in range(ni):
            for uv in range(2):
                asend[s, b, uv] = xbuf[:, uv * ni + b, :]

    project(0)
    send_all("img", lambda peer: asend.at[0, peer], lambda me, r: arecv.at[0, me], a_sem.at[0])
    arecv[0, ib] = asend[0, ib]
    project(1)
    send_all("img", lambda peer: asend.at[1, peer], lambda me, r: arecv.at[1, me], a_sem.at[1])
    arecv[1, ib] = asend[1, ib]
    loads[2].wait()
    halves = []

    for s in range(STEPS):
        def profiles(b):
            for t in range(TILES):
                g = b * TILES + t
                c = curve[0, pl.ds(g, 1), :]
                first = pl.multiple_of((b % SUBS) * SUB + t * 128, 128)
                d = pixels[...] - proj[b, 0, t : t + 1, :]
                pu[b // SUBS, :, pl.ds(first, 128)] = jnp.exp2(d * d * c).astype(jnp.bfloat16)
                d = pixels[...] - proj[b, 1, t : t + 1, :]
                pv[b // SUBS, :, pl.ds(first, 128)] = (
                    amp[pl.ds(g, 1), :] * jnp.exp2(d * d * c)
                ).astype(jnp.bfloat16)

        if s == 0:
            proj[ib] = arecv[0, ib]
            profiles(ib)
            wait_for(arecv.at[0, pl.ds(0, ni - 1)], a_sem.at[0, 1])
            proj[...] = arecv[0]
        else:
            wait_for(arecv.at[1, pl.ds(0, ni - 1)], a_sem.at[1, 1])
            proj[...] = arecv[1] - halves[0] * shift[...]

        def render(i, carry):
            profiles(lax.rem(ib + i, ni))
            return carry

        lax.fori_loop(1 if s == 0 else 0, ni, render, 0)

        image[...] = jnp.zeros_like(image)
        together = 4 if chunks % 4 == 0 else 1

        def add_image(i, carry):
            terms = [
                lax.dot_general(
                    pu[i * together + k],
                    pv[i * together + k],
                    (((1,), (1,)), ((), ())),
                    preferred_element_type=jnp.float32,
                )
                for k in range(together)
            ]
            image[...] += sum(terms)
            return carry

        lax.fori_loop(0, chunks // together, add_image, 0)

        for j in range(ng):
            isend[s, j] = image[j * rows : (j + 1) * rows, :].astype(isend.dtype)
        send_all(
            "gauss",
            lambda peer: isend.at[s, peer],
            lambda me, r: irecv.at[s, r - 1],
            i_sem.at[s],
        )
        if s == 0:
            loads[4].wait()
        measured = obs[chosen[s]].astype(jnp.float32)
        total = image[pl.ds(pl.multiple_of(gj * rows, rows), rows), :] - measured
        def slopes(b, carry):
            for t in range(TILES):
                first = pl.multiple_of((b % SUBS) * SUB + t * 128, 128)
                for uv, own, slope in ((0, pu, slope_u), (1, pv, slope_v)):
                    d = pixels[...] - proj[b, uv, t : t + 1, :]
                    slope[b // SUBS, :, pl.ds(first, 128)] = (
                        own[b // SUBS, :, pl.ds(first, 128)].astype(jnp.float32) * d
                    )
            return carry

        lax.fori_loop(0, ni, slopes, 0)
        cross = coefficients(s)[:, : 3 * K]
        other = jnp.concatenate([cross, psend[:, : 3 * K]], axis=0)
        wmat[...] = lax.dot_general(
            other,
            cross,
            (((1,), (1,)), ((), ())),
            precision=HIGH,
            preferred_element_type=jnp.float32,
        )
        for i in range(2 * ni):
            for k in range(i, 2 * ni):
                factor = 1.0 if i == k else 2.0
                weights[i, k] = jnp.broadcast_to(factor * wmat[i : i + 1, k : k + 1], (8, 128))
        if s == 0:
            for i in range(2 * ni):
                for uv in range(2):
                    at = 2 * ni + 2 + uv
                    weights[2 * ni + uv, i] = jnp.broadcast_to(
                        wmat[at : at + 1, i : i + 1], (8, 128)
                    )
        wait_for(irecv.at[s], i_sem.at[s, 1])
        for r in range(ng - 1):
            total = total + irecv[s, r].astype(jnp.float32)
        rsend[s] = total.astype(jnp.bfloat16)
        send_all("gauss", lambda peer: rsend.at[s], lambda me, r: whole.at[s, me], r_sem.at[s])
        whole[s, gj] = rsend[s]
        if s == STEPS - 1:
            final[...] = total
        wait_for(whole.at[s, pl.ds(0, ng - 1)], r_sem.at[s, 1])
        whole_t[0] = whole[s].reshape(PIX, PIX)
        whole_t[1] = whole_t[0].T

        def backward(c, carry):
            def part(k, carry):
                for half in range(2):
                    at = (2 * k + half) * BLK
                    cols = pl.ds(pl.multiple_of(at, BLK), BLK)
                    for uv, slope, matrix, other in (
                        (0, slope_u, whole_t[0], pv),
                        (1, slope_v, whole_t[1], pu),
                    ):
                        weighted = jnp.dot(
                            matrix, other[c, :, cols], preferred_element_type=jnp.float32
                        )
                        for t in range(BLK // 128):
                            tile = (2 * k + half) * (BLK // 128) + t
                            g = c * CTILES + tile
                            col = pl.ds(pl.multiple_of(at + t * 128, 128), 128)
                            total = slope[c, :, col] * weighted[:, t * 128 : (t + 1) * 128]
                            gown[pl.ds(uv * CTILES + tile, 1), :] = curve[
                                1, pl.ds(g, 1), :
                            ] * jnp.sum(total, axis=0, keepdims=True)
                return carry

            lax.fori_loop(0, CHUNK // (2 * BLK), part, 0)
            gsend[s, c] = gown[...].astype(jnp.bfloat16)
            send_all(
                "img",
                lambda peer: gsend.at[s, c],
                lambda me, r: grecv.at[s, c, me],
                g_sem.at[s, c],
            )
            grecv[s, c, ib] = gsend[s, c]
            return carry

        lax.fori_loop(0, chunks, backward, 0)

        def gradient(c, i):
            return gall[c, i % ni, (i // ni) * CTILES : (i // ni + 1) * CTILES, :]

        def add_squares(c, squares):
            wait_for(grecv.at[s, c, pl.ds(0, ni - 1)], g_sem.at[s, c, 1])
            gall[c] = grecv[s, c].astype(jnp.float32)
            for i in range(2 * ni):
                gi = gradient(c, i)
                for k in range(i, 2 * ni):
                    product = gi * gradient(c, k)
                    squares = squares + weights[i, k] * jnp.sum(
                        product.reshape(CTILES // 8, 8, 128), axis=0
                    )
            return squares

        squares = lax.fori_loop(0, chunks, add_squares, jnp.zeros((8, 128), jnp.float32))
        s2[s, gj] = jnp.sum(squares, axis=0, keepdims=True)
        send_all("gauss", lambda peer: s2.at[s, gj], lambda me, r: s2.at[s, me], s2_sem.at[s])
        if s == 0:

            def move(c, carry):
                for uv in range(2):
                    moved = jnp.zeros((SUBS, TILES, 128), jnp.float32)
                    for i in range(2 * ni):
                        moved = moved + weights[2 * ni + uv, i] * gradient(c, i).reshape(
                            SUBS, TILES, 128
                        )
                    shift[pl.ds(c * SUBS, SUBS), uv] = moved
                return carry

            lax.fori_loop(0, chunks, move, 0)
        for b in range(ni):
            for uv in range(2):
                first = pl.multiple_of(uv * CTILES + (ib % SUBS) * TILES, TILES)
                gpart[b, uv] = gall[ib // SUBS, b, pl.ds(first, TILES), :]
        for uv in range(2):
            for t in range(TILES):
                grads[uv * ni : (uv + 1) * ni, t * 128 : (t + 1) * 128] = gpart[:, uv, t, :]
        mgrad[s] = lax.dot_general(
            coefficients(s)[:, : 3 * K],
            grads[...],
            (((0,), (0,)), ((), ())),
            precision=HIGH,
            preferred_element_type=jnp.float32,
        )
        if s == 1:
            newv[...] = rows_in[: 3 * K, :] - halves[0] * mgrad[0]
        wait_for(s2.at[s, pl.ds(0, ng - 1)], s2_sem.at[s, 1])
        sums = jnp.sum(s2[s], axis=0)
        sums = jnp.sum(jnp.sum(sums, axis=0, keepdims=True), axis=1, keepdims=True)
        halves.append(step_size / jnp.sqrt(sums * (1.0 / entries) + tiny_eps))

    newv[...] = newv[...] - halves[1] * mgrad[1]

    wait_for(params.at[pl.ds(0, ni - 1)], p_sem.at[0])
    for s in range(STEPS):
        wait_for(arecv.at[s, pl.ds(0, ni - 1)], a_sem.at[s, 0])
        wait_for(irecv.at[s], i_sem.at[s, 0])
        wait_for(whole.at[s, pl.ds(0, ng - 1)], r_sem.at[s, 0])
        for c in range(chunks):
            wait_for(grecv.at[s, c, pl.ds(0, ni - 1)], g_sem.at[s, c, 0])
        wait_for(s2.at[s, pl.ds(0, ng - 1)], s2_sem.at[s, 0])


def body(
    observed, pose_index, batch_order, latents, base_positions, amplitudes, widths, deform_modes
):
    ng, ni = lax.axis_size("gauss"), lax.axis_size("img")
    rows = PIX // ng
    count = ni * SUB
    chunks = count // CHUNK
    f32, b16 = jnp.float32, jnp.bfloat16
    hbm, vmem = (pl.BlockSpec(memory_space=m) for m in (pltpu.HBM, pltpu.VMEM))
    held = functools.partial(pltpu.with_memory_space_constraint, memory_space=pltpu.HBM)
    dma = pltpu.SemaphoreType.DMA
    final, new = pl.pallas_call(
        functools.partial(kernel, ng, ni),
        out_shape=(
            jax.ShapeDtypeStruct((rows, PIX), f32),
            jax.ShapeDtypeStruct((3 * K, SUB), f32),
        ),
        in_specs=[hbm] * 8,
        out_specs=(vmem, vmem),
        scratch_shapes=[
            pltpu.SMEM(pose_index.shape, jnp.int32),
            pltpu.SMEM(batch_order.shape, jnp.int32),
            pltpu.VMEM(latents.shape, f32),
            pltpu.VMEM((8, 128), f32),
            pltpu.VMEM((4, rows, PIX), b16),
            pltpu.VMEM((3 * K + 8, SUB), f32),
            pltpu.VMEM((3, SUB), f32),
            pltpu.VMEM((count // 128, 128), f32),
            pltpu.VMEM((count // 128, 128), f32),
            pltpu.VMEM((2, count // 128, 128), f32),
            pltpu.VMEM((8, 128), f32),
            pltpu.VMEM((ni, 8, 128), f32),
            pltpu.VMEM((TILES, 2 * ni, 128), f32),
            pltpu.VMEM((STEPS, ni, 2, TILES, 128), f32),
            pltpu.VMEM((STEPS, ni, 2, TILES, 128), f32),
            pltpu.VMEM((ni, 2, TILES, 128), f32),
            pltpu.VMEM((2 * ni + 2, 2 * ni, 8, 128), f32),
            pltpu.VMEM((2 * ni + 8, 2 * ni), f32),
            pltpu.VMEM((ni, 2, TILES, 128), f32),
            pltpu.VMEM((PIX, 128), f32),
            pltpu.VMEM((chunks, PIX, CHUNK), b16),
            pltpu.VMEM((chunks, PIX, CHUNK), b16),
            pltpu.VMEM((chunks, PIX, CHUNK), f32),
            pltpu.VMEM((chunks, PIX, CHUNK), f32),
            pltpu.VMEM((PIX, PIX), f32),
            pltpu.VMEM((STEPS, ng, rows, PIX), b16),
            pltpu.VMEM((STEPS, ng - 1, rows, PIX), b16),
            pltpu.VMEM((STEPS, rows, PIX), b16),
            pltpu.VMEM((STEPS, ng, rows, PIX), b16),
            pltpu.VMEM((2, PIX, PIX), b16),
            pltpu.VMEM((2 * ni, SUB), f32),
            pltpu.VMEM((2 * CTILES, 128), f32),
            pltpu.VMEM((STEPS, chunks, 2 * CTILES, 128), b16),
            pltpu.VMEM((STEPS, chunks, ni, 2 * CTILES, 128), b16),
            pltpu.VMEM((chunks, ni, 2 * CTILES, 128), f32),
            pltpu.VMEM((ni, 2, TILES, 128), f32),
            pltpu.VMEM((STEPS, 3 * K, SUB), f32),
            pltpu.VMEM((STEPS, ng, 1, 128), f32),
            dma((8,)),
            dma((2,)),
            dma((STEPS, 2)),
            dma((STEPS, 2)),
            dma((STEPS, 2)),
            dma((STEPS, chunks, 2)),
            dma((STEPS, 2)),
        ],
        compiler_params=pltpu.CompilerParams(
            collective_id=0, has_side_effects=True, vmem_limit_bytes=40 * 2**20
        ),
    )(
        held(pose_index),
        held(batch_order),
        held(latents),
        held(observed),
        held(base_positions),
        held(amplitudes.reshape(count // 128, 128)),
        held(widths.reshape(count // 128, 128)),
        held(deform_modes.transpose(1, 0, 2).reshape(3 * K, SUB)),
    )
    return final[None], new.reshape(3, K, SUB).transpose(1, 0, 2)


def solution(mesh):
    return jax.shard_map(
        body,
        mesh=mesh,
        in_specs=(
            P("img", "gauss", None),
            P("img"),
            P("img"),
            P("img", None),
            P(None, "gauss"),
            P("gauss"),
            P("gauss"),
            P(None, None, ("gauss", "img")),
        ),
        out_specs=(P("img", "gauss", None), P(None, None, ("gauss", "img"))),
        check_vma=False,
    )
```

```python
import functools
import math

import jax
import jax.numpy as jnp
from jax import lax
from jax.experimental import pallas as pl
from jax.experimental.pallas import tpu as pltpu
from jax.sharding import PartitionSpec as P

PIX = 256
K = 16
NROT = 4096
STEPS = 2
SUB = 1024
TILES = SUB // 128
CHUNK = 2048
SUBS = CHUNK // SUB
CTILES = CHUNK // 128
BLK = 1024
CENTER = (PIX - 1) * 0.5

step_size = 0.5
tiny_eps = 1e-06
MESH = pl.DeviceIdType.MESH
HIGH = lax.Precision.HIGHEST


def cos_sin(units):
    quarter = (
        (units >= 18).astype(jnp.int32)
        + (units >= 54).astype(jnp.int32)
        + (units >= 90).astype(jnp.int32)
        + (units >= 126).astype(jnp.int32)
    )
    x = (units - 36 * quarter).astype(jnp.float32) * (2.0 * math.pi / 144.0)
    y = x * x
    s = x * (1.0 + y * (-1.0 / 6 + y * (1.0 / 120 + y * (-1.0 / 5040 + y * (1.0 / 362880)))))
    c = 1.0 + y * (
        -0.5 + y * (1.0 / 24 + y * (-1.0 / 720 + y * (1.0 / 40320 - y * (1.0 / 3628800))))
    )
    odd = (quarter == 1) | (quarter == 3)
    cos_a = jnp.where(odd, s, c)
    sin_a = jnp.where(odd, c, s)
    cos_a = jnp.where((quarter == 1) | (quarter == 2), -cos_a, cos_a)
    sin_a = jnp.where((quarter == 2) | (quarter == 3), -sin_a, sin_a)
    return cos_a, sin_a


def own_coefficients(pose, latent):
    lane = lax.broadcasted_iota(jnp.int32, (1, 128), 1)
    n = jnp.full((1, 128), pose, jnp.int32)
    cos_b = 1.0 - (2 * n + 1).astype(jnp.float32) * (1.0 / NROT)
    sin_b = jnp.sqrt(1.0 - cos_b * cos_b)
    cos_a, sin_a = cos_sin(jnp.full((1, 128), lax.rem(pose * 55, 144), jnp.int32))
    cos_g, sin_g = cos_sin(jnp.full((1, 128), lax.rem(pose, 8) * 18, jnp.int32))
    rows = (
        (
            cos_a * cos_b * cos_g - sin_a * sin_g,
            -cos_a * cos_b * sin_g - sin_a * cos_g,
            cos_a * sin_b,
        ),
        (
            sin_a * cos_b * cos_g + cos_a * sin_g,
            -sin_a * cos_b * sin_g + cos_a * cos_g,
            sin_a * sin_b,
        ),
    )
    spread = latent + pltpu.roll(latent, K, 1) + pltpu.roll(latent, 2 * K, 1)
    spread = jnp.where(lane < 3 * K, spread, jnp.where(lane < 3 * K + 3, 1.0, 0.0))
    first = (lane < K) | (lane == 3 * K)
    second = ((lane >= K) & (lane < 2 * K)) | (lane == 3 * K + 1)
    return [spread * jnp.where(first, r[0], jnp.where(second, r[1], r[2])) for r in rows]


def kernel(
    ng,
    ni,
    pose_hbm,
    order_hbm,
    lat_hbm,
    obs_hbm,
    base_hbm,
    amp_hbm,
    wid_hbm,
    modes_hbm,
    both,
    pose_ref,
    order_ref,
    lat_ref,
    zpad,
    obs,
    rows_in,
    base_in,
    amp,
    wid,
    curve,
    psend,
    params,
    xbuf,
    asend,
    arecv,
    shift,
    weights,
    wmat,
    proj,
    pixels,
    pu,
    pv,
    slope_u,
    slope_v,
    image,
    isend,
    irecv,
    rsend,
    whole,
    whole_t,
    grads,
    gown,
    gsend,
    grecv,
    gall,
    gpart,
    mgrad,
    s2,
    in_sem,
    p_sem,
    a_sem,
    i_sem,
    r_sem,
    g_sem,
    s2_sem,
):
    rows = PIX // ng
    chunks = ni * SUB // CHUNK
    entries = 3 * K * SUB * ni * ng
    gj = lax.axis_index("gauss")
    ib = lax.axis_index("img")

    def partner(axis, n, r):
        me = ib if axis == "img" else gj
        return lax.rem(me + (n // 2 + r if r < n // 2 else n - r), n)

    barrier = pltpu.get_barrier_semaphore()
    for axis, n in (("gauss", ng), ("img", ni)):
        for r in range(1, n):
            pl.semaphore_signal(
                barrier, inc=1, device_id={axis: partner(axis, n, r)}, device_id_type=MESH
            )

    loads = [
        pltpu.make_async_copy(pose_hbm, pose_ref, in_sem.at[5]),
        pltpu.make_async_copy(order_hbm, order_ref, in_sem.at[6]),
        pltpu.make_async_copy(lat_hbm, lat_ref, in_sem.at[7]),
        pltpu.make_async_copy(modes_hbm, rows_in.at[pl.ds(0, 3 * K)], in_sem.at[0]),
        pltpu.make_async_copy(
            base_hbm.at[:, pl.ds(pl.multiple_of(ib * SUB, SUB), SUB)], base_in, in_sem.at[1]
        ),
        pltpu.make_async_copy(amp_hbm, amp, in_sem.at[2]),
        pltpu.make_async_copy(wid_hbm, wid, in_sem.at[3]),
        pltpu.make_async_copy(obs_hbm, obs, in_sem.at[4]),
    ]
    for copy in loads:
        copy.start()

    for copy in loads[:3]:
        copy.wait()
    del loads[:3]
    zpad[...] = jnp.zeros_like(zpad)
    zpad[0:4, 0:K] = lat_ref[...]
    chosen = [order_ref[s] for s in range(STEPS)]
    psend[...] = jnp.zeros_like(psend)
    for s in range(STEPS):
        pair = own_coefficients(pose_ref[chosen[s]], zpad[pl.ds(chosen[s], 1), :])
        psend[2 * s : 2 * s + 1, :] = pair[0]
        psend[2 * s + 1 : 2 * s + 2, :] = pair[1]
    params[ib] = psend[...]

    pl.semaphore_wait(barrier, ni + ng - 2)

    def send_all(axis, source, target, sem):
        me, n = (ib, ni) if axis == "img" else (gj, ng)
        for r in range(1, n):
            peer = partner(axis, n, r)
            pltpu.make_async_remote_copy(
                src_ref=source(peer),
                dst_ref=target(me, r),
                send_sem=sem.at[0],
                recv_sem=sem.at[1],
                device_id={axis: peer},
                device_id_type=MESH,
            ).start()

    def wait_for(part, sem):
        pltpu.make_async_copy(part, part, sem).wait()

    send_all("img", lambda peer: psend, lambda me, r: params.at[me], p_sem)

    pixels[...] = lax.broadcasted_iota(jnp.int32, (PIX, 128), 0).astype(jnp.float32)
    loads[0].wait()
    loads[1].wait()
    rows_in[3 * K :, :] = jnp.zeros_like(rows_in[3 * K :, :])
    rows_in[3 * K : 3 * K + 3, :] = base_in[...]
    loads[3].wait()
    w = wid[...]
    inv = 1.0 / (w * w)
    curve[1] = inv
    curve[0] = inv * (-0.5 * math.log2(math.e))

    wait_for(params.at[pl.ds(0, ni - 1)], p_sem.at[1])

    def coefficients(s):
        return jnp.concatenate([params[:, 2 * s, :], params[:, 2 * s + 1, :]], axis=0)

    def project(s):
        got = lax.dot_general(
            coefficients(s)[:, : 3 * K + 8],
            rows_in[...],
            (((1,), (0,)), ((), ())),
            precision=HIGH,
            preferred_element_type=jnp.float32,
        )
        got = got + CENTER
        for t in range(TILES):
            xbuf[t] = got[:, t * 128 : (t + 1) * 128]
        for b in range(ni):
            for uv in range(2):
                asend[s, b, uv] = xbuf[:, uv * ni + b, :]

    project(0)
    send_all("img", lambda peer: asend.at[0, peer], lambda me, r: arecv.at[0, me], a_sem.at[0])
    arecv[0, ib] = asend[0, ib]
    project(1)
    send_all("img", lambda peer: asend.at[1, peer], lambda me, r: arecv.at[1, me], a_sem.at[1])
    arecv[1, ib] = asend[1, ib]
    loads[2].wait()
    halves = []

    for s in range(STEPS):
        def side_by_side(ref, first, n):
            return jnp.concatenate([ref[first + t] for t in range(n)], axis=1)

        def profiles(b):
            for t in range(TILES):
                g = b * TILES + t
                c = curve[0, pl.ds(g, 1), :]
                u, v = proj[b, 0, t : t + 1, :], proj[b, 1, t : t + 1, :]
                a = amp[pl.ds(g, 1), :]
                for m in range(0, PIX, 16):
                    part = slice(m, m + 16)
                    d = pixels[part] - u
                    pu[g, part] = jnp.exp2(d * d * c).astype(jnp.bfloat16)
                    d = pixels[part] - v
                    pv[g, part] = (a * jnp.exp2(d * d * c)).astype(jnp.bfloat16)

        if s == 0:
            proj[ib] = arecv[0, ib]
            profiles(ib)
            wait_for(arecv.at[0, pl.ds(0, ni - 1)], a_sem.at[0, 1])
            proj[...] = arecv[0]
        else:
            wait_for(arecv.at[1, pl.ds(0, ni - 1)], a_sem.at[1, 1])
            proj[...] = arecv[1] - halves[0] * shift[...]

        def render(i, carry):
            profiles(lax.rem(ib + i, ni))
            return carry

        lax.fori_loop(1 if s == 0 else 0, ni, render, 0)

        image[...] = jnp.zeros_like(image)
        together = 4 if chunks % 4 == 0 else 1

        def add_image(i, carry):
            terms = [
                lax.dot_general(
                    side_by_side(pu, (i * together + k) * CTILES, CTILES),
                    side_by_side(pv, (i * together + k) * CTILES, CTILES),
                    (((1,), (1,)), ((), ())),
                    preferred_element_type=jnp.float32,
                )
                for k in range(together)
            ]
            image[...] += sum(terms)
            return carry

        lax.fori_loop(0, chunks // together, add_image, 0)

        for j in range(ng):
            isend[s, j] = image[j * rows : (j + 1) * rows, :].astype(isend.dtype)
        send_all(
            "gauss",
            lambda peer: isend.at[s, peer],
            lambda me, r: irecv.at[s, r - 1],
            i_sem.at[s],
        )
        if s == 0:
            loads[4].wait()
        measured = obs[chosen[s]].astype(jnp.float32)
        total = image[pl.ds(pl.multiple_of(gj * rows, rows), rows), :] - measured
        def slopes(b, carry):
            for t in range(TILES):
                g = b * TILES + t
                for uv, own, slope in ((0, pu, slope_u), (1, pv, slope_v)):
                    d = pixels[...] - proj[b, uv, t : t + 1, :]
                    slope[g] = own[g].astype(jnp.float32) * d
            return carry

        lax.fori_loop(0, ni, slopes, 0)
        cross = coefficients(s)[:, : 3 * K]
        other = jnp.concatenate([cross, psend[:, : 3 * K]], axis=0)
        wmat[...] = lax.dot_general(
            other,
            cross,
            (((1,), (1,)), ((), ())),
            precision=HIGH,
            preferred_element_type=jnp.float32,
        )
        for i in range(2 * ni):
            for k in range(i, 2 * ni):
                factor = 1.0 if i == k else 2.0
                weights[i, k] = jnp.broadcast_to(factor * wmat[i : i + 1, k : k + 1], (8, 128))
        if s == 0:
            for i in range(2 * ni):
                for uv in range(2):
                    at = 2 * ni + 2 + uv
                    weights[2 * ni + uv, i] = jnp.broadcast_to(
                        wmat[at : at + 1, i : i + 1], (8, 128)
                    )
        wait_for(irecv.at[s], i_sem.at[s, 1])
        for r in range(ng - 1):
            total = total + irecv[s, r].astype(jnp.float32)
        rsend[s] = total.astype(jnp.bfloat16)
        send_all("gauss", lambda peer: rsend.at[s], lambda me, r: whole.at[s, me], r_sem.at[s])
        whole[s, gj] = rsend[s]
        if s == STEPS - 1:
            both[3 * K :, :PIX] = total
        wait_for(whole.at[s, pl.ds(0, ng - 1)], r_sem.at[s, 1])
        whole_t[0] = whole[s].reshape(PIX, PIX)
        whole_t[1] = whole_t[0].T

        def backward(c, carry):
            def part(k, carry):
                for half in range(2):
                    at = (2 * k + half) * (BLK // 128)
                    for uv, slope, matrix, other in (
                        (0, slope_u, whole_t[0], pv),
                        (1, slope_v, whole_t[1], pu),
                    ):
                        weighted = jnp.dot(
                            matrix,
                            side_by_side(other, c * CTILES + at, BLK // 128),
                            preferred_element_type=jnp.float32
                        )
                        for t in range(BLK // 128):
                            tile = at + t
                            g = c * CTILES + tile
                            total = slope[g] * weighted[:, t * 128 : (t + 1) * 128]
                            gown[pl.ds(uv * CTILES + tile, 1), :] = curve[
                                1, pl.ds(g, 1), :
                            ] * jnp.sum(total, axis=0, keepdims=True)
                return carry

            lax.fori_loop(0, CHUNK // (2 * BLK), part, 0)
            gsend[s, c] = gown[...].astype(jnp.bfloat16)
            send_all(
                "img",
                lambda peer: gsend.at[s, c],
                lambda me, r: grecv.at[s, c, me],
                g_sem.at[s, c],
            )
            grecv[s, c, ib] = gsend[s, c]
            return carry

        lax.fori_loop(0, chunks, backward, 0)

        def gradient(c, i):
            return gall[c, i % ni, (i // ni) * CTILES : (i // ni + 1) * CTILES, :]

        def add_squares(c, squares):
            wait_for(grecv.at[s, c, pl.ds(0, ni - 1)], g_sem.at[s, c, 1])
            gall[c] = grecv[s, c].astype(jnp.float32)
            for i in range(2 * ni):
                gi = gradient(c, i)
                for k in range(i, 2 * ni):
                    product = gi * gradient(c, k)
                    squares = squares + weights[i, k] * jnp.sum(
                        product.reshape(CTILES // 8, 8, 128), axis=0
                    )
            return squares

        squares = lax.fori_loop(0, chunks, add_squares, jnp.zeros((8, 128), jnp.float32))
        s2[s, gj] = jnp.sum(squares, axis=0, keepdims=True)
        send_all("gauss", lambda peer: s2.at[s, gj], lambda me, r: s2.at[s, me], s2_sem.at[s])
        if s == 0:

            def move(c, carry):
                for uv in range(2):
                    moved = jnp.zeros((SUBS, TILES, 128), jnp.float32)
                    for i in range(2 * ni):
                        moved = moved + weights[2 * ni + uv, i] * gradient(c, i).reshape(
                            SUBS, TILES, 128
                        )
                    shift[pl.ds(c * SUBS, SUBS), uv] = moved
                return carry

            lax.fori_loop(0, chunks, move, 0)
        for b in range(ni):
            for uv in range(2):
                first = pl.multiple_of(uv * CTILES + (ib % SUBS) * TILES, TILES)
                gpart[b, uv] = gall[ib // SUBS, b, pl.ds(first, TILES), :]
        for uv in range(2):
            for t in range(TILES):
                grads[uv * ni : (uv + 1) * ni, t * 128 : (t + 1) * 128] = gpart[:, uv, t, :]
        mgrad[s] = lax.dot_general(
            coefficients(s)[:, : 3 * K],
            grads[...],
            (((0,), (0,)), ((), ())),
            precision=HIGH,
            preferred_element_type=jnp.float32,
        )
        if s == 1:
            both[: 3 * K, :] = rows_in[: 3 * K, :] - halves[0] * mgrad[0]
        wait_for(s2.at[s, pl.ds(0, ng - 1)], s2_sem.at[s, 1])
        sums = jnp.sum(s2[s], axis=0)
        sums = jnp.sum(jnp.sum(sums, axis=0, keepdims=True), axis=1, keepdims=True)
        halves.append(step_size / jnp.sqrt(sums * (1.0 / entries) + tiny_eps))

    both[: 3 * K, :] = both[: 3 * K, :] - halves[1] * mgrad[1]

    wait_for(params.at[pl.ds(0, ni - 1)], p_sem.at[0])
    for s in range(STEPS):
        wait_for(arecv.at[s, pl.ds(0, ni - 1)], a_sem.at[s, 0])
        wait_for(irecv.at[s], i_sem.at[s, 0])
        wait_for(whole.at[s, pl.ds(0, ng - 1)], r_sem.at[s, 0])
        for c in range(chunks):
            wait_for(grecv.at[s, c, pl.ds(0, ni - 1)], g_sem.at[s, c, 0])
        wait_for(s2.at[s, pl.ds(0, ng - 1)], s2_sem.at[s, 0])


def body(
    observed, pose_index, batch_order, latents, base_positions, amplitudes, widths, deform_modes
):
    ng, ni = lax.axis_size("gauss"), lax.axis_size("img")
    rows = PIX // ng
    count = ni * SUB
    chunks = count // CHUNK
    f32, b16 = jnp.float32, jnp.bfloat16
    hbm, vmem = (pl.BlockSpec(memory_space=m) for m in (pltpu.HBM, pltpu.VMEM))
    held = functools.partial(pltpu.with_memory_space_constraint, memory_space=pltpu.HBM)
    dma = pltpu.SemaphoreType.DMA
    both = pl.pallas_call(
        functools.partial(kernel, ng, ni),
        out_shape=jax.ShapeDtypeStruct((3 * K + rows, SUB), f32),
        in_specs=[hbm] * 8,
        out_specs=vmem,
        scratch_shapes=[
            pltpu.SMEM(pose_index.shape, jnp.int32),
            pltpu.SMEM(batch_order.shape, jnp.int32),
            pltpu.VMEM(latents.shape, f32),
            pltpu.VMEM((8, 128), f32),
            pltpu.VMEM((4, rows, PIX), b16),
            pltpu.VMEM((3 * K + 8, SUB), f32),
            pltpu.VMEM((3, SUB), f32),
            pltpu.VMEM((count // 128, 128), f32),
            pltpu.VMEM((count // 128, 128), f32),
            pltpu.VMEM((2, count // 128, 128), f32),
            pltpu.VMEM((8, 128), f32),
            pltpu.VMEM((ni, 8, 128), f32),
            pltpu.VMEM((TILES, 2 * ni, 128), f32),
            pltpu.VMEM((STEPS, ni, 2, TILES, 128), f32),
            pltpu.VMEM((STEPS, ni, 2, TILES, 128), f32),
            pltpu.VMEM((ni, 2, TILES, 128), f32),
            pltpu.VMEM((2 * ni + 2, 2 * ni, 8, 128), f32),
            pltpu.VMEM((2 * ni + 8, 2 * ni), f32),
            pltpu.VMEM((ni, 2, TILES, 128), f32),
            pltpu.VMEM((PIX, 128), f32),
            pltpu.VMEM((count // 128, PIX, 128), b16),
            pltpu.VMEM((count // 128, PIX, 128), b16),
            pltpu.VMEM((count // 128, PIX, 128), f32),
            pltpu.VMEM((count // 128, PIX, 128), f32),
            pltpu.VMEM((PIX, PIX), f32),
            pltpu.VMEM((STEPS, ng, rows, PIX), b16),
            pltpu.VMEM((STEPS, ng - 1, rows, PIX), b16),
            pltpu.VMEM((STEPS, rows, PIX), b16),
            pltpu.VMEM((STEPS, ng, rows, PIX), b16),
            pltpu.VMEM((2, PIX, PIX), b16),
            pltpu.VMEM((2 * ni, SUB), f32),
            pltpu.VMEM((2 * CTILES, 128), f32),
            pltpu.VMEM((STEPS, chunks, 2 * CTILES, 128), b16),
            pltpu.VMEM((STEPS, chunks, ni, 2 * CTILES, 128), b16),
            pltpu.VMEM((chunks, ni, 2 * CTILES, 128), f32),
            pltpu.VMEM((ni, 2, TILES, 128), f32),
            pltpu.VMEM((STEPS, 3 * K, SUB), f32),
            pltpu.VMEM((STEPS, ng, 1, 128), f32),
            dma((8,)),
            dma((2,)),
            dma((STEPS, 2)),
            dma((STEPS, 2)),
            dma((STEPS, 2)),
            dma((STEPS, chunks, 2)),
            dma((STEPS, 2)),
        ],
        compiler_params=pltpu.CompilerParams(
            collective_id=0, has_side_effects=True, vmem_limit_bytes=40 * 2**20
        ),
    )(
        held(pose_index),
        held(batch_order),
        held(latents),
        held(observed),
        held(base_positions),
        held(amplitudes.reshape(count // 128, 128)),
        held(widths.reshape(count // 128, 128)),
        held(deform_modes.transpose(1, 0, 2).reshape(3 * K, SUB)),
    )
    new = both[: 3 * K].reshape(3, K, SUB).transpose(1, 0, 2)
    return both[None, 3 * K :, :PIX], new


def solution(mesh):
    return jax.shard_map(
        body,
        mesh=mesh,
        in_specs=(
            P("img", "gauss", None),
            P("img"),
            P("img"),
            P("img", None),
            P(None, "gauss"),
            P("gauss"),
            P("gauss"),
            P(None, None, ("gauss", "img")),
        ),
        out_specs=(P("img", "gauss", None), P(None, None, ("gauss", "img"))),
        check_vma=False,
    )
```

```python
import functools
import math

import jax
import jax.numpy as jnp
from jax import lax
from jax.experimental import pallas as pl
from jax.experimental.pallas import tpu as pltpu
from jax.sharding import PartitionSpec as P

PIX = 256
K = 16
NROT = 4096
STEPS = 2
SUB = 1024
TILES = SUB // 128
CHUNK = 2048
SUBS = CHUNK // SUB
CTILES = CHUNK // 128
BLK = 1024
CENTER = (PIX - 1) * 0.5

step_size = 0.5
tiny_eps = 1e-06
MESH = pl.DeviceIdType.MESH
HIGH = lax.Precision.HIGHEST


def cos_sin(units):
    quarter = (
        (units >= 18).astype(jnp.int32)
        + (units >= 54).astype(jnp.int32)
        + (units >= 90).astype(jnp.int32)
        + (units >= 126).astype(jnp.int32)
    )
    x = (units - 36 * quarter).astype(jnp.float32) * (2.0 * math.pi / 144.0)
    y = x * x
    s = x * (1.0 + y * (-1.0 / 6 + y * (1.0 / 120 + y * (-1.0 / 5040 + y * (1.0 / 362880)))))
    c = 1.0 + y * (
        -0.5 + y * (1.0 / 24 + y * (-1.0 / 720 + y * (1.0 / 40320 - y * (1.0 / 3628800))))
    )
    odd = (quarter == 1) | (quarter == 3)
    cos_a = jnp.where(odd, s, c)
    sin_a = jnp.where(odd, c, s)
    cos_a = jnp.where((quarter == 1) | (quarter == 2), -cos_a, cos_a)
    sin_a = jnp.where((quarter == 2) | (quarter == 3), -sin_a, sin_a)
    return cos_a, sin_a


def own_coefficients(pose, latent):
    lane = lax.broadcasted_iota(jnp.int32, (1, 128), 1)
    n = jnp.full((1, 128), pose, jnp.int32)
    cos_b = 1.0 - (2 * n + 1).astype(jnp.float32) * (1.0 / NROT)
    sin_b = jnp.sqrt(1.0 - cos_b * cos_b)
    cos_a, sin_a = cos_sin(jnp.full((1, 128), lax.rem(pose * 55, 144), jnp.int32))
    cos_g, sin_g = cos_sin(jnp.full((1, 128), lax.rem(pose, 8) * 18, jnp.int32))
    rows = (
        (
            cos_a * cos_b * cos_g - sin_a * sin_g,
            -cos_a * cos_b * sin_g - sin_a * cos_g,
            cos_a * sin_b,
        ),
        (
            sin_a * cos_b * cos_g + cos_a * sin_g,
            -sin_a * cos_b * sin_g + cos_a * cos_g,
            sin_a * sin_b,
        ),
    )
    spread = latent + pltpu.roll(latent, K, 1) + pltpu.roll(latent, 2 * K, 1)
    spread = jnp.where(lane < 3 * K, spread, jnp.where(lane < 3 * K + 3, 1.0, 0.0))
    first = (lane < K) | (lane == 3 * K)
    second = ((lane >= K) & (lane < 2 * K)) | (lane == 3 * K + 1)
    return [spread * jnp.where(first, r[0], jnp.where(second, r[1], r[2])) for r in rows]


def kernel(
    ng,
    ni,
    pose_hbm,
    order_hbm,
    lat_hbm,
    obs_hbm,
    base_hbm,
    amp_hbm,
    wid_hbm,
    modes_hbm,
    both,
    pose_ref,
    order_ref,
    lat_ref,
    zpad,
    obs,
    rows_in,
    base_in,
    amp,
    wid,
    curve,
    psend,
    params,
    xbuf,
    asend,
    arecv,
    shift,
    weights,
    wmat,
    proj,
    pixels,
    pu,
    pv,
    slope_u,
    slope_v,
    image,
    isend,
    irecv,
    rsend,
    whole,
    whole_t,
    grads,
    gown,
    gsend,
    grecv,
    gall,
    gpart,
    mgrad,
    s2,
    in_sem,
    p_sem,
    a_sem,
    i_sem,
    r_sem,
    g_sem,
    s2_sem,
):
    rows = PIX // ng
    chunks = ni * SUB // CHUNK
    entries = 3 * K * SUB * ni * ng
    gj = lax.axis_index("gauss")
    ib = lax.axis_index("img")

    def partner(axis, n, r):
        me = ib if axis == "img" else gj
        return lax.rem(me + (n // 2 + r if r < n // 2 else n - r), n)

    barrier = pltpu.get_barrier_semaphore()
    for axis, n in (("gauss", ng), ("img", ni)):
        for r in range(1, n):
            pl.semaphore_signal(
                barrier, inc=1, device_id={axis: partner(axis, n, r)}, device_id_type=MESH
            )

    loads = [
        pltpu.make_async_copy(pose_hbm, pose_ref, in_sem.at[5]),
        pltpu.make_async_copy(order_hbm, order_ref, in_sem.at[6]),
        pltpu.make_async_copy(lat_hbm, lat_ref, in_sem.at[7]),
        pltpu.make_async_copy(modes_hbm, rows_in.at[pl.ds(0, 3 * K)], in_sem.at[0]),
        pltpu.make_async_copy(
            base_hbm.at[:, pl.ds(pl.multiple_of(ib * SUB, SUB), SUB)], base_in, in_sem.at[1]
        ),
        pltpu.make_async_copy(amp_hbm, amp, in_sem.at[2]),
        pltpu.make_async_copy(wid_hbm, wid, in_sem.at[3]),
        pltpu.make_async_copy(obs_hbm, obs, in_sem.at[4]),
    ]
    for copy in loads:
        copy.start()

    for copy in loads[:3]:
        copy.wait()
    del loads[:3]
    zpad[...] = jnp.zeros_like(zpad)
    zpad[0:4, 0:K] = lat_ref[...]
    chosen = [order_ref[s] for s in range(STEPS)]
    psend[...] = jnp.zeros_like(psend)
    for s in range(STEPS):
        pair = own_coefficients(pose_ref[chosen[s]], zpad[pl.ds(chosen[s], 1), :])
        psend[2 * s : 2 * s + 1, :] = pair[0]
        psend[2 * s + 1 : 2 * s + 2, :] = pair[1]
    params[ib] = psend[...]

    pl.semaphore_wait(barrier, ni + ng - 2)

    def send_all(axis, source, target, sem):
        me, n = (ib, ni) if axis == "img" else (gj, ng)
        for r in range(1, n):
            peer = partner(axis, n, r)
            pltpu.make_async_remote_copy(
                src_ref=source(peer),
                dst_ref=target(me, r),
                send_sem=sem.at[0],
                recv_sem=sem.at[1],
                device_id={axis: peer},
                device_id_type=MESH,
            ).start()

    def wait_for(part, sem):
        pltpu.make_async_copy(part, part, sem).wait()

    send_all("img", lambda peer: psend, lambda me, r: params.at[me], p_sem)

    pixels[...] = lax.broadcasted_iota(jnp.int32, (PIX, 128), 0).astype(jnp.float32)
    loads[0].wait()
    loads[1].wait()
    rows_in[3 * K :, :] = jnp.zeros_like(rows_in[3 * K :, :])
    rows_in[3 * K : 3 * K + 3, :] = base_in[...]
    loads[3].wait()
    w = wid[...]
    inv = 1.0 / (w * w)
    curve[1] = inv
    curve[0] = inv * (-0.5 * math.log2(math.e))

    wait_for(params.at[pl.ds(0, ni - 1)], p_sem.at[1])

    def coefficients(s):
        return jnp.concatenate([params[:, 2 * s, :], params[:, 2 * s + 1, :]], axis=0)

    def project(s):
        got = lax.dot_general(
            coefficients(s)[:, : 3 * K + 8],
            rows_in[...],
            (((1,), (0,)), ((), ())),
            precision=HIGH,
            preferred_element_type=jnp.float32,
        )
        got = got + CENTER
        for t in range(TILES):
            xbuf[t] = got[:, t * 128 : (t + 1) * 128]
        for b in range(ni):
            for uv in range(2):
                asend[s, b, uv] = xbuf[:, uv * ni + b, :]

    project(0)
    send_all("img", lambda peer: asend.at[0, peer], lambda me, r: arecv.at[0, me], a_sem.at[0])
    arecv[0, ib] = asend[0, ib]
    project(1)
    send_all("img", lambda peer: asend.at[1, peer], lambda me, r: arecv.at[1, me], a_sem.at[1])
    arecv[1, ib] = asend[1, ib]
    loads[2].wait()
    halves = []

    for s in range(STEPS):
        def side_by_side(ref, first, n):
            return jnp.concatenate([ref[first + t] for t in range(n)], axis=1)

        def profiles(b):
            for t in range(TILES):
                g = b * TILES + t
                c = curve[0, pl.ds(g, 1), :]
                u, v = proj[b, 0, t : t + 1, :], proj[b, 1, t : t + 1, :]
                a = amp[pl.ds(g, 1), :]
                for m in range(0, PIX, 16):
                    part = slice(m, m + 16)
                    d = pixels[part] - u
                    pu[g, part] = jnp.exp2(d * d * c).astype(jnp.bfloat16)
                    d = pixels[part] - v
                    pv[g, part] = (a * jnp.exp2(d * d * c)).astype(jnp.bfloat16)

        if s == 0:
            proj[ib] = arecv[0, ib]
            profiles(ib)
            wait_for(arecv.at[0, pl.ds(0, ni - 1)], a_sem.at[0, 1])
            proj[...] = arecv[0]
        else:
            wait_for(arecv.at[1, pl.ds(0, ni - 1)], a_sem.at[1, 1])
            proj[...] = arecv[1] - halves[0] * shift[...]

        def render(i, carry):
            profiles(lax.rem(ib + i, ni))
            return carry

        lax.fori_loop(1 if s == 0 else 0, ni, render, 0)

        image[...] = jnp.zeros_like(image)
        together = 4 if chunks % 4 == 0 else 1

        def add_image(i, carry):
            terms = [
                lax.dot_general(
                    side_by_side(pu, (i * together + k) * CTILES, CTILES),
                    side_by_side(pv, (i * together + k) * CTILES, CTILES),
                    (((1,), (1,)), ((), ())),
                    preferred_element_type=jnp.float32,
                )
                for k in range(together)
            ]
            image[...] += sum(terms)
            return carry

        lax.fori_loop(0, chunks // together, add_image, 0)

        for j in range(ng):
            isend[s, j] = image[j * rows : (j + 1) * rows, :].astype(isend.dtype)
        send_all(
            "gauss",
            lambda peer: isend.at[s, peer],
            lambda me, r: irecv.at[s, r - 1],
            i_sem.at[s],
        )
        if s == 0:
            loads[4].wait()
        measured = obs[chosen[s]].astype(jnp.float32)
        total = image[pl.ds(pl.multiple_of(gj * rows, rows), rows), :] - measured
        def slopes(b, carry):
            for t in range(TILES):
                g = b * TILES + t
                for uv, own, slope in ((0, pu, slope_u), (1, pv, slope_v)):
                    d = pixels[...] - proj[b, uv, t : t + 1, :]
                    slope[g] = own[g].astype(jnp.float32) * d
            return carry

        lax.fori_loop(0, ni, slopes, 0)
        cross = coefficients(s)[:, : 3 * K]
        other = jnp.concatenate([cross, psend[:, : 3 * K]], axis=0)
        wmat[...] = lax.dot_general(
            other,
            cross,
            (((1,), (1,)), ((), ())),
            precision=HIGH,
            preferred_element_type=jnp.float32,
        )
        for i in range(2 * ni):
            for k in range(i, 2 * ni):
                factor = 1.0 if i == k else 2.0
                weights[i, k] = jnp.broadcast_to(factor * wmat[i : i + 1, k : k + 1], (8, 128))
        if s == 0:
            for i in range(2 * ni):
                for uv in range(2):
                    at = 2 * ni + 2 + uv
                    weights[2 * ni + uv, i] = jnp.broadcast_to(
                        wmat[at : at + 1, i : i + 1], (8, 128)
                    )
        wait_for(irecv.at[s], i_sem.at[s, 1])
        for r in range(ng - 1):
            total = total + irecv[s, r].astype(jnp.float32)
        rsend[s] = total.astype(jnp.bfloat16)
        send_all("gauss", lambda peer: rsend.at[s], lambda me, r: whole.at[s, me], r_sem.at[s])
        whole[s, gj] = rsend[s]
        if s == STEPS - 1:
            both[3 * K :, :PIX] = total
        wait_for(whole.at[s, pl.ds(0, ng - 1)], r_sem.at[s, 1])
        whole_t[...] = whole[s].reshape(PIX, PIX).T

        def backward(c, carry):
            def part(k, carry):
                for half in range(2):
                    at = (2 * k + half) * (BLK // 128)
                    for uv, slope, matrix, other in (
                        (0, slope_u, whole[s].reshape(PIX, PIX), pv),
                        (1, slope_v, whole_t[...], pu),
                    ):
                        weighted = jnp.dot(
                            matrix,
                            side_by_side(other, c * CTILES + at, BLK // 128),
                            preferred_element_type=jnp.float32
                        )
                        for t in range(BLK // 128):
                            tile = at + t
                            g = c * CTILES + tile
                            total = slope[g] * weighted[:, t * 128 : (t + 1) * 128]
                            gown[pl.ds(uv * CTILES + tile, 1), :] = curve[
                                1, pl.ds(g, 1), :
                            ] * jnp.sum(total, axis=0, keepdims=True)
                return carry

            lax.fori_loop(0, CHUNK // (2 * BLK), part, 0)
            gsend[s, c] = gown[...].astype(jnp.bfloat16)
            send_all(
                "img",
                lambda peer: gsend.at[s, c],
                lambda me, r: grecv.at[s, c, me],
                g_sem.at[s, c],
            )
            grecv[s, c, ib] = gsend[s, c]
            return carry

        lax.fori_loop(0, chunks, backward, 0)

        def gradient(c, i):
            return gall[c, i % ni, (i // ni) * CTILES : (i // ni + 1) * CTILES, :]

        def add_squares(c, squares):
            wait_for(grecv.at[s, c, pl.ds(0, ni - 1)], g_sem.at[s, c, 1])
            gall[c] = grecv[s, c].astype(jnp.float32)
            for i in range(2 * ni):
                gi = gradient(c, i)
                for k in range(i, 2 * ni):
                    product = gi * gradient(c, k)
                    squares = squares + weights[i, k] * jnp.sum(
                        product.reshape(CTILES // 8, 8, 128), axis=0
                    )
            return squares

        squares = lax.fori_loop(0, chunks, add_squares, jnp.zeros((8, 128), jnp.float32))
        s2[s, gj] = jnp.sum(squares, axis=0, keepdims=True)
        send_all("gauss", lambda peer: s2.at[s, gj], lambda me, r: s2.at[s, me], s2_sem.at[s])
        if s == 0:

            def move(c, carry):
                for uv in range(2):
                    moved = jnp.zeros((SUBS, TILES, 128), jnp.float32)
                    for i in range(2 * ni):
                        moved = moved + weights[2 * ni + uv, i] * gradient(c, i).reshape(
                            SUBS, TILES, 128
                        )
                    shift[pl.ds(c * SUBS, SUBS), uv] = moved
                return carry

            lax.fori_loop(0, chunks, move, 0)
        for b in range(ni):
            for uv in range(2):
                first = pl.multiple_of(uv * CTILES + (ib % SUBS) * TILES, TILES)
                gpart[b, uv] = gall[ib // SUBS, b, pl.ds(first, TILES), :]
        for uv in range(2):
            for t in range(TILES):
                grads[uv * ni : (uv + 1) * ni, t * 128 : (t + 1) * 128] = gpart[:, uv, t, :]
        mgrad[s] = lax.dot_general(
            coefficients(s)[:, : 3 * K],
            grads[...],
            (((0,), (0,)), ((), ())),
            precision=HIGH,
            preferred_element_type=jnp.float32,
        )
        if s == 1:
            both[: 3 * K, :] = rows_in[: 3 * K, :] - halves[0] * mgrad[0]
        wait_for(s2.at[s, pl.ds(0, ng - 1)], s2_sem.at[s, 1])
        sums = jnp.sum(s2[s], axis=0)
        sums = jnp.sum(jnp.sum(sums, axis=0, keepdims=True), axis=1, keepdims=True)
        halves.append(step_size / jnp.sqrt(sums * (1.0 / entries) + tiny_eps))

    both[: 3 * K, :] = both[: 3 * K, :] - halves[1] * mgrad[1]

    wait_for(params.at[pl.ds(0, ni - 1)], p_sem.at[0])
    for s in range(STEPS):
        wait_for(arecv.at[s, pl.ds(0, ni - 1)], a_sem.at[s, 0])
        wait_for(irecv.at[s], i_sem.at[s, 0])
        wait_for(whole.at[s, pl.ds(0, ng - 1)], r_sem.at[s, 0])
        for c in range(chunks):
            wait_for(grecv.at[s, c, pl.ds(0, ni - 1)], g_sem.at[s, c, 0])
        wait_for(s2.at[s, pl.ds(0, ng - 1)], s2_sem.at[s, 0])


def body(
    observed, pose_index, batch_order, latents, base_positions, amplitudes, widths, deform_modes
):
    ng, ni = lax.axis_size("gauss"), lax.axis_size("img")
    rows = PIX // ng
    count = ni * SUB
    chunks = count // CHUNK
    f32, b16 = jnp.float32, jnp.bfloat16
    hbm, vmem = (pl.BlockSpec(memory_space=m) for m in (pltpu.HBM, pltpu.VMEM))
    held = functools.partial(pltpu.with_memory_space_constraint, memory_space=pltpu.HBM)
    dma = pltpu.SemaphoreType.DMA
    both = pl.pallas_call(
        functools.partial(kernel, ng, ni),
        out_shape=jax.ShapeDtypeStruct((3 * K + rows, SUB), f32),
        in_specs=[hbm] * 8,
        out_specs=vmem,
        scratch_shapes=[
            pltpu.SMEM(pose_index.shape, jnp.int32),
            pltpu.SMEM(batch_order.shape, jnp.int32),
            pltpu.VMEM(latents.shape, f32),
            pltpu.VMEM((8, 128), f32),
            pltpu.VMEM((4, rows, PIX), b16),
            pltpu.VMEM((3 * K + 8, SUB), f32),
            pltpu.VMEM((3, SUB), f32),
            pltpu.VMEM((count // 128, 128), f32),
            pltpu.VMEM((count // 128, 128), f32),
            pltpu.VMEM((2, count // 128, 128), f32),
            pltpu.VMEM((8, 128), f32),
            pltpu.VMEM((ni, 8, 128), f32),
            pltpu.VMEM((TILES, 2 * ni, 128), f32),
            pltpu.VMEM((STEPS, ni, 2, TILES, 128), f32),
            pltpu.VMEM((STEPS, ni, 2, TILES, 128), f32),
            pltpu.VMEM((ni, 2, TILES, 128), f32),
            pltpu.VMEM((2 * ni + 2, 2 * ni, 8, 128), f32),
            pltpu.VMEM((2 * ni + 8, 2 * ni), f32),
            pltpu.VMEM((ni, 2, TILES, 128), f32),
            pltpu.VMEM((PIX, 128), f32),
            pltpu.VMEM((count // 128, PIX, 128), b16),
            pltpu.VMEM((count // 128, PIX, 128), b16),
            pltpu.VMEM((count // 128, PIX, 128), f32),
            pltpu.VMEM((count // 128, PIX, 128), f32),
            pltpu.VMEM((PIX, PIX), f32),
            pltpu.VMEM((STEPS, ng, rows, PIX), b16),
            pltpu.VMEM((STEPS, ng - 1, rows, PIX), b16),
            pltpu.VMEM((STEPS, rows, PIX), b16),
            pltpu.VMEM((STEPS, ng, rows, PIX), b16),
            pltpu.VMEM((PIX, PIX), b16),
            pltpu.VMEM((2 * ni, SUB), f32),
            pltpu.VMEM((2 * CTILES, 128), f32),
            pltpu.VMEM((STEPS, chunks, 2 * CTILES, 128), b16),
            pltpu.VMEM((STEPS, chunks, ni, 2 * CTILES, 128), b16),
            pltpu.VMEM((chunks, ni, 2 * CTILES, 128), f32),
            pltpu.VMEM((ni, 2, TILES, 128), f32),
            pltpu.VMEM((STEPS, 3 * K, SUB), f32),
            pltpu.VMEM((STEPS, ng, 1, 128), f32),
            dma((8,)),
            dma((2,)),
            dma((STEPS, 2)),
            dma((STEPS, 2)),
            dma((STEPS, 2)),
            dma((STEPS, chunks, 2)),
            dma((STEPS, 2)),
        ],
        compiler_params=pltpu.CompilerParams(
            collective_id=0, has_side_effects=True, vmem_limit_bytes=40 * 2**20
        ),
    )(
        held(pose_index),
        held(batch_order),
        held(latents),
        held(observed),
        held(base_positions),
        held(amplitudes.reshape(count // 128, 128)),
        held(widths.reshape(count // 128, 128)),
        held(deform_modes.transpose(1, 0, 2).reshape(3 * K, SUB)),
    )
    new = both[: 3 * K].reshape(3, K, SUB).transpose(1, 0, 2)
    return both[None, 3 * K :, :PIX], new


def solution(mesh):
    return jax.shard_map(
        body,
        mesh=mesh,
        in_specs=(
            P("img", "gauss", None),
            P("img"),
            P("img"),
            P("img", None),
            P(None, "gauss"),
            P("gauss"),
            P("gauss"),
            P(None, None, ("gauss", "img")),
        ),
        out_specs=(P("img", "gauss", None), P(None, None, ("gauss", "img"))),
        check_vma=False,
    )
```
